512 devices in a mesh: seq: 64 (over x, y, core), head: 8 (over z).
Axes of the slice: x: 4, y: 8, z: 8, core: 2. Of those that a mesh axis runs over, the one named last changes fastest.
Arguments:
- queries: bfloat16 [128, 8192], P('seq', 'head'), may hold values from -12 to 12
- prefix_keys: bfloat16 [262144, 1024], P('seq', 'head'), may hold values from -6 to 6
- prefix_values: bfloat16 [262144, 1024], P('seq', 'head'), may hold values from -12 to 12
- suffix_keys: bfloat16 [128, 2048, 1024], P('seq', None, 'head'), may hold values from -8.375 to 8.375
- suffix_values: bfloat16 [128, 2048, 1024], P('seq', None, 'head'), may hold values from -12 to 12
- suffix_length: int32 [128], P('seq'), may hold values from 1 to 2048, 131072 in all
- slot_answer: int32 [128], P('seq'), may hold values from 0 to 127, each once
Outputs:
- attended: bfloat16 [128, 8192], P('seq')
The draws below stay inside these ranges and needn't reach their ends.
Inputs may be any that keep to these rules, and one draw needn't show every extreme that they name: `suffix_length`: the longest suffix has exactly 2048 live positions. `slot_answer`: every answer is held by exactly one slot.
All inputs are finite; a program needn't handle non-finite values. No bound on the sum of `suffix_length` on one device may be relied on, other than what follows from the above.
Results may differ from the reference program's by a relative error of at most 0.005.
Values may be sent and summed in bfloat16 or wider, within the bound.
A program may use at most 64 MiB of HBM per device.

```python
import math
import jax
import jax.numpy as jnp
import numpy as np
from jax import lax

QH = 64
KVH = 8
HD = 128
SUF = 2048
ANS = 128
PRE = 262144


def shared_signs(key):
    return jnp.where(jax.random.bernoulli(key, 0.5, (KVH, HD)), 1.0, -1.0).astype(jnp.float32)


def aligned_queries(values, signs):
    spread = jnp.broadcast_to(signs[:, None, :], (KVH, QH // KVH, HD)).reshape(1, QH * HD)
    count = min(3, ANS)
    strength = jnp.array([10.0, 11.0, 12.0], jnp.float32)[:count]
    return values.at[:count].set(strength[:, None] * spread)


def aligned_keys(values, signs):
    flat = signs.reshape(KVH, HD)
    near = 2.0 * math.sqrt(HD) / 11.0
    second = flat.at[:, 0].set(flat[:, 0] * (5.8 - near) / 5.8)
    values = values.at[PRE - 1:PRE].set(5.8 * flat.reshape(1, KVH * HD))
    values = values.at[PRE - 2:PRE - 1].set(5.8 * second.reshape(1, KVH * HD))
    return values


def draw_queries(key, part):
    signs = shared_signs(key)
    key = jax.random.fold_in(key, 11)
    values = jnp.clip(3.0 * jax.random.normal(key, (ANS, QH * HD), jnp.float32), -12.0, 12.0)
    return aligned_queries(values, signs).astype(jnp.bfloat16)


def draw_prefix_keys(key, part):
    signs = shared_signs(key)
    key = jax.random.fold_in(key, 23)
    values = jnp.clip(jax.random.normal(key, (PRE, KVH * HD), jnp.float32), -6.0, 6.0)
    return aligned_keys(values, signs).astype(jnp.bfloat16)


def level_of(key, dims, shards, smallest, high):
    gain, own = 1.0, jax.random.fold_in(key, 6)
    for axis_at, parts in shards:
        steps = jnp.exp(jax.random.uniform(jax.random.fold_in(own, axis_at), (parts,), jnp.float32, smallest / len(shards), high / len(shards)))
        gain = gain * jnp.repeat(steps, dims[axis_at] // parts).reshape([-1 if axis == axis_at else 1 for axis in range(len(dims))])
    return gain


def length_profile(number_of, total, reach, slope):
    portions = [(1 << 20) // math.isqrt(grade ** slope) + 1 for grade in range(2, number_of + 1)]
    spare, counts = total - reach - (number_of - 1), [1] * (number_of - 1)
    while spare > 0:
        movable = [i for i in range(number_of - 1) if counts[i] < reach]
        mass, left = sum([portions[i] for i in movable]), spare
        for i in movable:
            extra = min(reach - counts[i], max(1, left * portions[i] // mass), spare)
            counts[i] = counts[i] + extra
            spare = spare - extra
    return np.array([reach] + counts)


def ragged_sizes(rng, amount, total, limit, skew):
    if amount == 2:
        one = jax.random.randint(rng, (), max(1, total - limit), min(limit, total - 1) + 1)
        return jnp.stack([one, total - one])
    tallies = jnp.asarray(length_profile(amount, total, limit, skew), jnp.int32)
    twos = (amount - 1) // 2
    giver, receiver = tallies[1:1 + 2 * twos:2], tallies[2:2 + 2 * twos:2]
    margin = jnp.minimum(giver - 1, limit - receiver)
    moved = jax.random.randint(jax.random.fold_in(rng, 1), (twos,), 0, 1 << 20) % (margin + 1)
    tallies = tallies.at[1:1 + 2 * twos:2].set(giver - moved).at[2:2 + 2 * twos:2].set(receiver + moved)
    return tallies[jax.random.permutation(jax.random.fold_in(rng, 2), amount)]


def scatter_about(stream_key, extent, scale, bound, shards=(), kind=jnp.bfloat16):
    drawn = jax.random.normal(stream_key, extent, jnp.float32) * scale
    if len(shards) > 0:
        drawn = level_of(stream_key, extent, shards, -0.22, 0.18) * drawn
    return jnp.clip(drawn, min=-bound, max=bound).astype(kind)


def setup_inputs(seed: int = 0) -> dict:
    splits = jax.random.split(jax.random.key(seed), 8)
    queries = draw_queries(jax.random.fold_in(splits[7], 71), 0)
    prefix_keys = draw_prefix_keys(jax.random.fold_in(splits[7], 71), 0)
    prefix_values = scatter_about(splits[2], (PRE, KVH * HD), 2.0, 12.0, ((0, 64), (1, 8)))
    suffix_keys = scatter_about(splits[3], (ANS, SUF, KVH * HD), 1.4, 8.375, ((0, 64), (2, 8)))
    suffix_values = scatter_about(splits[4], (ANS, SUF, KVH * HD), 2.0, 12.0, ((0, 64), (2, 8)))
    suffix_length = ragged_sizes(splits[5], ANS, ANS * SUF // 2, SUF, 2).astype(jnp.int32)
    slot_answer = jax.random.permutation(splits[6], ANS).astype(jnp.int32)
    return {"queries": queries, "prefix_keys": prefix_keys, "prefix_values": prefix_values, "suffix_keys": suffix_keys, "suffix_values": suffix_values, "suffix_length": suffix_length, "slot_answer": slot_answer}


NEG_BIG = -1e+30

def reference(queries, prefix_keys, prefix_values, suffix_keys, suffix_values, suffix_length, slot_answer):
    per_group = QH // KVH
    score_scale = 1.0 / math.sqrt(HD)
    answers = queries.shape[0]
    owner_slot = jnp.zeros((answers,), jnp.int32).at[slot_answer].set(jnp.arange(answers, dtype=jnp.int32))
    batch = math.gcd(answers, max(1, 128 // per_group))
    slot_blocks = owner_slot.reshape(answers // batch, batch)
    pieces_out = []
    for head_group in range(KVH):
        start = head_group * per_group * HD
        query_blocks = queries[:, start:start + per_group * HD].reshape(answers // batch, batch, per_group, HD)
        key_block = prefix_keys[:, head_group * HD:(head_group + 1) * HD]
        value_block = prefix_values[:, head_group * HD:(head_group + 1) * HD]

        def one_block(pieces, head_group=head_group, key_block=key_block, value_block=value_block):
            query_piece, slot_piece = pieces
            flat_rows = query_piece.reshape(batch * per_group, HD)
            pre_scores = lax.dot_general(flat_rows, key_block, (((1,), (1,)), ((), ())), preferred_element_type=jnp.float32) * score_scale
            slot_keys = jnp.take(suffix_keys, slot_piece, axis=0)[:, :, head_group * HD:(head_group + 1) * HD]
            slot_values = jnp.take(suffix_values, slot_piece, axis=0)[:, :, head_group * HD:(head_group + 1) * HD]
            lengths = jnp.take(suffix_length, slot_piece, axis=0)
            live_mask = jnp.arange(SUF, dtype=jnp.int32)[None, :] < lengths[:, None]
            suf_scores = jnp.einsum('ahd,akd->ahk', query_piece.astype(jnp.float32), slot_keys.astype(jnp.float32)) * score_scale
            suf_scores = jnp.where(live_mask[:, None, :], suf_scores, NEG_BIG)
            top = jnp.maximum(lax.optimization_barrier(jnp.max(pre_scores, axis=1)).reshape(batch, per_group), lax.optimization_barrier(jnp.max(suf_scores, axis=2)))
            pre_weights = jnp.exp(pre_scores - top.reshape(batch * per_group)[:, None])
            suf_weights = jnp.where(live_mask[:, None, :], jnp.exp(suf_scores - top[:, :, None]), 0.0)
            total = lax.optimization_barrier(jnp.sum(pre_weights, axis=1)).reshape(batch, per_group) + lax.optimization_barrier(jnp.sum(suf_weights, axis=2))
            pre_sum = jnp.dot(pre_weights.astype(jnp.bfloat16), value_block, preferred_element_type=jnp.float32).reshape(batch, per_group, HD)
            suf_sum = jnp.einsum('ahk,akd->ahd', suf_weights.astype(jnp.bfloat16).astype(jnp.float32), slot_values.astype(jnp.float32))
            return ((pre_sum + suf_sum) / total[:, :, None]).astype(jnp.bfloat16)
        result = lax.map(one_block, (query_blocks, slot_blocks))
        pieces_out.append(result.reshape(answers, per_group * HD))
    return jnp.concatenate(pieces_out, axis=1)
```

```python
import functools
import math

import jax
import jax.numpy as jnp
from jax import lax
from jax.experimental import pallas as pl
from jax.experimental.pallas import tpu as pltpu
from jax.sharding import PartitionSpec as P

HD = 128
PER_GROUP = 8
NEG_BIG = -1e30
EXP2_SCALE = math.log2(math.e) / math.sqrt(HD)
ROWS = 16
F32 = jnp.float32
BF16 = jnp.bfloat16
MESH = pl.DeviceIdType.MESH


def attend(x_chips, y_chips, z_chips, chunk, q_ref, pk, pv, sk, sv, slen, sans, out_ref, qbuf, kraw, kt, vbuf, skb, svb,
           sbuf, own, give, take, slot, msg, got, zbuf, local_sem, qsend, qrecv, fsend, frecv, psend, precv, msend, mrecv, zsend, zrecv):
    seq, z = lax.axis_index("seq"), lax.axis_index("head")
    core, chip = seq % 2, seq // 2
    x, y = chip // y_chips, chip % y_chips
    sibling = chip * 2 + 1 - core
    chips = x_chips * y_chips
    unit_rows = y_chips * ROWS
    keys = kraw.shape[0]

    def device(xx, yy):
        return (xx * y_chips + yy) * 2 + core

    copies = [
        pltpu.make_async_copy(pk, kraw, local_sem.at[0]),
        pltpu.make_async_copy(pv, vbuf, local_sem.at[1]),
        pltpu.make_async_copy(sk, skb, local_sem.at[2]),
        pltpu.make_async_copy(sv, svb, local_sem.at[3]),
        pltpu.make_async_copy(q_ref, qbuf.at[y], local_sem.at[4]),
    ]

    barrier = pltpu.get_barrier_semaphore()
    pl.semaphore_signal(barrier, inc=1, device_id=(sibling, z), device_id_type=MESH)

    @pl.loop(1, chips)
    def _(step):
        pl.semaphore_signal(barrier, inc=1, device_id=((chip + step) % chips * 2 + core, z), device_id_type=MESH)

    @pl.loop(1, z_chips)
    def _(step):
        pl.semaphore_signal(barrier, inc=1, device_id=(seq, (z + step) % z_chips), device_id_type=MESH)

    for copy in copies:
        copy.start()
    pl.semaphore_wait(barrier, 1 + (chips - 1) + (z_chips - 1))

    def send_queries(group, step):
        return pltpu.make_async_remote_copy(
            src_ref=q_ref,
            dst_ref=qbuf.at[group * y_chips + y],
            send_sem=qsend,
            recv_sem=qrecv.at[group],
            device_id=(device((x + x_chips - group) % x_chips, (y + step) % y_chips), z),
            device_id_type=MESH,
        )

    for group in range(x_chips):

        @pl.loop(1 if group == 0 else 0, y_chips)
        def _(step, group=group):
            send_queries(group, step).start()

    copies[0].wait()

    @pl.loop(0, keys // chunk)
    def _(step):
        at = pl.multiple_of(step * chunk, chunk)
        kt[:, pl.ds(at, chunk)] = kraw[pl.ds(at, chunk), :].T

    copies[4].wait()
    copies[1].wait()

    def await_queries(group):
        first = 1 if group == 0 else 0
        part = qbuf.at[pl.ds(group * y_chips, y_chips - first)]
        pltpu.make_async_remote_copy(
            src_ref=part, dst_ref=part, send_sem=qsend, recv_sem=qrecv.at[group], device_id=(sibling, z), device_id_type=MESH
        ).wait_recv()

    def forward(part):
        begin, count = ((0, 1), (1, x_chips - 1))[part]
        return pltpu.make_async_remote_copy(
            src_ref=qbuf.at[pl.ds(begin * y_chips, count * y_chips)],
            dst_ref=qbuf.at[pl.ds((x_chips + begin) * y_chips, count * y_chips)],
            send_sem=fsend.at[part],
            recv_sem=frecv.at[part],
            device_id=(sibling, z),
            device_id_type=MESH,
        )

    def partials(group):
        return pltpu.make_async_remote_copy(
            src_ref=give.at[group],
            dst_ref=take.at[group],
            send_sem=psend.at[group],
            recv_sem=precv.at[group],
            device_id=(sibling, z),
            device_id_type=MESH,
        )

    def stabiliser(scores_top):
        top = jnp.max(scores_top, axis=1, keepdims=True) * EXP2_SCALE
        return top.astype(BF16).astype(F32)

    def lane_tiles_max(scores):
        tiles = [scores[:, at : at + 128] for at in range(0, scores.shape[1], 128)]
        return functools.reduce(jnp.maximum, tiles)

    def weighted(scores, top, values):
        weights = jnp.exp2(scores * EXP2_SCALE - top).astype(BF16)
        wide = jnp.concatenate([values, jnp.ones(values.shape, BF16)], axis=1)
        return jnp.dot(weights, wide, preferred_element_type=F32)

    def suffix(at):
        holder = sans[at] // 2
        unit = (holder + core) % 2 * x_chips + (holder // (2 * y_chips) - x + x_chips) % x_chips
        rows = qbuf[unit * y_chips + holder // 2 % y_chips]
        scores = lax.dot_general(rows, skb[at], (((1,), (1,)), ((), ())), preferred_element_type=F32)
        position = lax.broadcasted_iota(jnp.int32, scores.shape, 1)
        scores = jnp.where(position < slen[at], scores, NEG_BIG)
        top = stabiliser(lane_tiles_max(scores))
        both = weighted(scores, top, svb[at])
        slot[at, 0] = both[:, :HD]
        slot[at, 1] = both[:, HD:]
        slot[at, 2] = jnp.broadcast_to(top, (ROWS, HD))

    def merged(first, second):
        top = jnp.maximum(first[2], second[2])
        one, two = jnp.exp2(first[2] - top), jnp.exp2(second[2] - top)
        return first[0] * one + second[0] * two, first[1] * one + second[1] * two, top

    def with_slots(part, unit):
        shape = (y_chips, ROWS, HD)
        xx = (x + unit % x_chips) % x_chips
        row = lax.broadcasted_iota(jnp.int32, shape, 1)
        answer = (xx * y_chips + lax.broadcasted_iota(jnp.int32, shape, 0)) * 4 + (core + unit // x_chips) % 2 * 2 + row // PER_GROUP
        part = tuple(value.reshape(shape) for value in part)
        for at in range(2):
            hit = answer == sans[at]
            piece = [jnp.broadcast_to(slot[at, which][None], shape) for which in range(3)]
            part = merged(part, (piece[0], piece[1], jnp.where(hit, piece[2], NEG_BIG)))
        return tuple(value.reshape(unit_rows, HD) for value in part)

    lane = lax.broadcasted_iota(jnp.int32, (unit_rows, HD), 1)

    def send_group(group):
        mine = tuple(own[group, which] for which in range(3))
        mine = with_slots(mine, group)
        stats = take[group, 1]
        theirs = (
            take[group, 0],
            jnp.broadcast_to(stats[:, 64:65], (unit_rows, HD)),
            jnp.broadcast_to(stats[:, 0:1], (unit_rows, HD)),
        )
        total_sum, total, top = merged(mine, theirs)
        high = total.astype(BF16).astype(F32)
        stats = jnp.where(lane < 32, top, jnp.where(lane < 64, high, total - high))
        blocks = pl.ds(group * y_chips, y_chips)
        msg[blocks, 0:ROWS, :] = total_sum.astype(BF16).reshape(y_chips, ROWS, HD)
        msg[blocks, ROWS : 2 * ROWS, :] = stats.astype(BF16).reshape(y_chips, ROWS, HD)

        def send(step):
            yy = (y + step) % y_chips
            pltpu.make_async_remote_copy(
                src_ref=msg.at[group * y_chips + yy],
                dst_ref=got.at[(x_chips - group) % x_chips * y_chips + y],
                send_sem=msend,
                recv_sem=mrecv,
                device_id=(device((x + group) % x_chips, yy), z),
                device_id_type=MESH,
            ).start()

        pl.loop(1, y_chips)(send)

        @pl.when(group != 0)
        def _():
            send(0)

        @pl.when(group == 0)
        def _():
            got[y] = msg[y]

    @pl.loop(0, 2 * x_chips)
    def _(turn):
        unit = turn + 2 * ((turn + 6) // 8) - 6 * ((turn + 2) // 8)

        @pl.when(turn == 0)
        def _():
            await_queries(0)
            forward(0).start()

        @pl.when(turn == 1)
        def _():
            for group in range(1, x_chips):
                await_queries(group)
            forward(1).start()

        @pl.when(turn == 2)
        def _():
            forward(0).wait_recv()
            forward(1).wait_recv()
            copies[2].wait()
            copies[3].wait()
            for at in range(2):
                suffix(at)

        rows = qbuf[pl.ds(unit * y_chips, y_chips)].reshape(unit_rows, HD)
        top = None
        for at in range(0, keys, chunk):
            scores = jnp.dot(rows, kt[:, at : at + chunk], preferred_element_type=F32)
            sbuf[:, at : at + chunk] = scores
            here = lane_tiles_max(scores)
            top = here if top is None else jnp.maximum(top, here)
        top = stabiliser(top)
        both = jnp.zeros((unit_rows, 2 * HD), F32)
        for at in range(0, keys, chunk):
            both += weighted(sbuf[:, at : at + chunk], top, vbuf[at : at + chunk, :])
        part = (both[:, :HD], both[:, HD:], jnp.broadcast_to(top, (unit_rows, HD)))

        @pl.when(unit < x_chips)
        def _():
            for which in range(3):
                own[unit, which] = part[which]

        @pl.when(unit >= x_chips)
        def _():
            total_sum, total, highest = with_slots(part, unit)
            give[unit - x_chips, 0] = total_sum
            give[unit - x_chips, 1] = jnp.where(lane < 64, highest, total)
            partials(unit - x_chips).start()

        @pl.when(turn >= 3)
        def _():
            @pl.when(turn != 5)
            def _():
                group = turn - 3 - turn // 6
                partials(group).wait_recv()
                send_group(group)

    def whole(ref, count, send_sem, recv_sem):
        part = ref.at[pl.ds(0, count)]
        return pltpu.make_async_remote_copy(
            src_ref=part, dst_ref=part, send_sem=send_sem, recv_sem=recv_sem, device_id=(sibling, z), device_id_type=MESH
        )

    whole(got, chips - 1, msend, mrecv).wait_recv()
    sums = got[:, 0:ROWS, :].astype(F32)
    stats = got[:, ROWS : 2 * ROWS, :].astype(F32)
    shape = sums.shape
    tops = jnp.broadcast_to(stats[:, :, 0:1], shape)
    totals = jnp.broadcast_to(stats[:, :, 32:33], shape) + jnp.broadcast_to(stats[:, :, 64:65], shape)
    factor = jnp.exp2(tops - jnp.max(tops, axis=0, keepdims=True))
    result = jnp.sum(sums * factor, axis=0) / jnp.sum(totals * factor, axis=0)
    zbuf[z] = result.astype(BF16)

    @pl.loop(1, z_chips)
    def _(step):
        pltpu.make_async_remote_copy(
            src_ref=zbuf.at[z],
            dst_ref=zbuf.at[z],
            send_sem=zsend,
            recv_sem=zrecv,
            device_id=(seq, (z + step) % z_chips),
            device_id_type=MESH,
        ).start()

    whole(qbuf, chips - 1, qsend, mrecv).wait_send()
    forward(0).wait_send()
    forward(1).wait_send()
    for group in range(x_chips):
        partials(group).wait_send()
    whole(msg, chips - 1, msend, mrecv).wait_send()
    heads = whole(zbuf, z_chips - 1, zsend, zrecv)
    heads.wait_recv()
    out_ref[...] = zbuf[...]
    heads.wait_send()


def on_device(x_chips, queries, prefix_keys, prefix_values, suffix_keys, suffix_values, suffix_length, slot_answer):
    z_chips = lax.axis_size("head")
    chips = lax.axis_size("seq") // 2
    y_chips = chips // x_chips
    keys, cap = prefix_keys.shape[0], suffix_keys.shape[1]
    unit_rows = y_chips * ROWS
    chunk = min(512, keys)
    hbm = pl.BlockSpec(memory_space=pltpu.MemorySpace.HBM)
    vmem = pl.BlockSpec(memory_space=pltpu.VMEM)
    smem = pl.BlockSpec(memory_space=pltpu.SMEM)
    dma = pltpu.SemaphoreType.DMA
    heads = pl.pallas_call(
        functools.partial(attend, x_chips, y_chips, z_chips, chunk),
        out_shape=jax.ShapeDtypeStruct((z_chips, ROWS, HD), BF16),
        in_specs=[vmem, hbm, hbm, hbm, hbm, smem, smem],
        out_specs=vmem,
        scratch_shapes=[
            pltpu.VMEM((2 * chips, ROWS, HD), BF16),
            pltpu.VMEM((keys, HD), BF16),
            pltpu.VMEM((HD, keys), BF16),
            pltpu.VMEM((keys, HD), BF16),
            pltpu.VMEM((2, cap, HD), BF16),
            pltpu.VMEM((2, cap, HD), BF16),
            pltpu.VMEM((unit_rows, keys), F32),
            pltpu.VMEM((x_chips, 3, unit_rows, HD), F32),
            pltpu.VMEM((x_chips, 2, unit_rows, HD), F32),
            pltpu.VMEM((x_chips, 2, unit_rows, HD), F32),
            pltpu.VMEM((2, 3, ROWS, HD), F32),
            pltpu.VMEM((chips, 2 * ROWS, HD), BF16),
            pltpu.VMEM((chips, 2 * ROWS, HD), BF16),
            pltpu.VMEM((z_chips, ROWS, HD), BF16),
            dma((5,)),
            dma,
            dma((x_chips,)),
            dma((2,)),
            dma((2,)),
            dma((x_chips,)),
            dma((x_chips,)),
            dma,
            dma,
            dma,
            dma,
        ],
        compiler_params=pltpu.CompilerParams(collective_id=0, has_side_effects=True, vmem_limit_bytes=48 << 20),
        name="attend",
    )(
        queries.reshape(ROWS, HD),
        prefix_keys,
        prefix_values,
        suffix_keys,
        suffix_values,
        suffix_length,
        slot_answer,
    )
    heads = heads.reshape(z_chips, 2, PER_GROUP * HD)
    return jnp.swapaxes(heads, 0, 1).reshape(2, z_chips * PER_GROUP * HD)


def solution(mesh):
    in_specs = (
        P("seq", "head"),
        P("seq", "head"),
        P("seq", "head"),
        P("seq", None, "head"),
        P("seq", None, "head"),
        P("seq"),
        P("seq"),
    )
    return jax.shard_map(
        functools.partial(on_device, 4), mesh=mesh, in_specs=in_specs, out_specs=P("seq", None), check_vma=False
    )
```

```python
import functools
import math

import jax
import jax.numpy as jnp
from jax import lax
from jax.experimental import pallas as pl
from jax.experimental.pallas import tpu as pltpu
from jax.sharding import PartitionSpec as P

HD = 128
PER_GROUP = 8
NEG_BIG = -1e30
EXP2_SCALE = math.log2(math.e) / math.sqrt(HD)
ROWS = 16
F32 = jnp.float32
BF16 = jnp.bfloat16
MESH = pl.DeviceIdType.MESH


def attend(x_chips, y_chips, z_chips, chunk, q_ref, pk, pv, sk, sv, slen, sans, out_ref, qraw, qown, qbuf, kraw, kt, vbuf, skb, svb,
           even, odd, own, give, take, slot, msg, got, zbuf, local_sem, qsend, qrecv, fsend, frecv, psend, precv, msend, mrecv, zsend, zrecv):
    seq, z = lax.axis_index("seq"), lax.axis_index("head")
    chip = seq // 2
    core = seq - chip * 2
    x = chip // y_chips
    y = chip - x * y_chips
    sibling = chip * 2 + 1 - core
    chips = x_chips * y_chips
    half = chips // 2
    unit_rows = half * ROWS
    keys = kraw.shape[0]

    def start_others(begin, count, me, start):
        @pl.loop(begin, begin + count)
        def _(at):
            @pl.when(at != me)
            def _():
                start(at)

    copies = [
        pltpu.make_async_copy(pk, kraw, local_sem.at[0]),
        pltpu.make_async_copy(pv, vbuf, local_sem.at[1]),
        pltpu.make_async_copy(sk, skb, local_sem.at[2]),
        pltpu.make_async_copy(sv, svb, local_sem.at[3]),
    ]
    query_copy = pltpu.make_async_copy(q_ref, qraw, local_sem.at[4])
    query_copy.start()

    barrier = pltpu.get_barrier_semaphore()

    def greet(to):
        pl.semaphore_signal(barrier, inc=1, device_id=to, device_id_type=MESH)

    start_others(0, chips, chip, lambda at: greet((at * 2 + core, z)))
    greet((sibling, z))
    start_others(0, z_chips, z, lambda at: greet((seq, at)))
    for copy in copies:
        copy.start()

    query_copy.wait()
    raw = qraw[...].astype(F32)
    pieces = [raw[at : at + 1, h * HD : (h + 1) * HD] for at in range(2) for h in range(PER_GROUP)]
    block = jnp.concatenate(pieces, axis=0).astype(BF16)
    qown[...] = block
    qbuf[y] = block
    pl.semaphore_wait(barrier, 1 + (chips - 1) + (z_chips - 1))

    for group in range(x_chips):
        column = (x + x_chips - group) % x_chips * y_chips

        def send_queries(yy, group=group, column=column):
            pltpu.make_async_remote_copy(
                src_ref=qown,
                dst_ref=qbuf.at[group * y_chips + y],
                send_sem=qsend,
                recv_sem=qrecv.at[group],
                device_id=((column + yy) * 2 + core, z),
                device_id_type=MESH,
            ).start()

        if group == 0:
            start_others(0, y_chips, y, send_queries)
        else:
            pl.loop(0, y_chips)(send_queries)

    copies[0].wait()

    @pl.loop(0, keys // chunk)
    def _(step):
        at = pl.multiple_of(step * chunk, chunk)
        kt[:, pl.ds(at, chunk)] = kraw[pl.ds(at, chunk), :].T

    def await_queries(group):
        first = 1 if group == 0 else 0
        part = qbuf.at[pl.ds(group * y_chips, y_chips - first)]
        pltpu.make_async_remote_copy(
            src_ref=part, dst_ref=part, send_sem=qsend, recv_sem=qrecv.at[group], device_id=(sibling, z), device_id_type=MESH
        ).wait_recv()

    def forward(part):
        return pltpu.make_async_remote_copy(
            src_ref=qbuf.at[pl.ds(part * half, half)],
            dst_ref=qbuf.at[pl.ds(chips + part * half, half)],
            send_sem=fsend.at[part],
            recv_sem=frecv.at[part],
            device_id=(sibling, z),
            device_id_type=MESH,
        )

    def partials(part):
        return pltpu.make_async_remote_copy(
            src_ref=give.at[part],
            dst_ref=take.at[part],
            send_sem=psend.at[part],
            recv_sem=precv.at[part],
            device_id=(sibling, z),
            device_id_type=MESH,
        )

    def stabiliser(scores_top):
        top = jnp.max(scores_top, axis=1, keepdims=True) * EXP2_SCALE
        return top.astype(BF16).astype(F32)

    def lane_tiles_max(scores):
        tiles = [scores[:, at : at + 128] for at in range(0, scores.shape[1], 128)]
        return functools.reduce(jnp.maximum, tiles)

    def weighted(scores, top, values):
        weights = jnp.exp2(scores * EXP2_SCALE - top).astype(BF16)
        wide = jnp.concatenate([values, jnp.ones(values.shape, BF16)], axis=1)
        return jnp.dot(weights, wide, preferred_element_type=F32)

    def turn(now, top, begin, later):
        both, later_top = None, None
        rows = None if begin is None else qbuf[begin : begin + half].reshape(unit_rows, HD)
        for at in range(0, keys, chunk):
            if begin is not None:
                scores = jnp.dot(rows, kt[:, at : at + chunk], preferred_element_type=F32)
                later[:, at : at + chunk] = scores
                here = lane_tiles_max(scores)
                later_top = here if later_top is None else jnp.maximum(later_top, here)
            if now is not None:
                here = weighted(now[:, at : at + chunk], top, vbuf[at : at + chunk, :])
                both = here if both is None else both + here
        part = None if now is None else (both[:, :HD], both[:, HD:], jnp.broadcast_to(top, (unit_rows, HD)))
        return part, None if begin is None else stabiliser(later_top)

    def suffix(at):
        holder = sans[at] // 2
        block = (holder + core) % 2 * chips + (holder // 2 - x * y_chips + chips) % chips
        scores = lax.dot_general(qbuf[block], skb[at], (((1,), (1,)), ((), ())), preferred_element_type=F32)
        position = lax.broadcasted_iota(jnp.int32, scores.shape, 1)
        scores = jnp.where(position < slen[at], scores, NEG_BIG)
        top = stabiliser(lane_tiles_max(scores))
        both = weighted(scores, top, svb[at])
        slot[at, 0] = both[:, :HD]
        slot[at, 1] = both[:, HD:]
        slot[at, 2] = jnp.broadcast_to(top, (ROWS, HD))

    def merged(first, second):
        top = jnp.maximum(first[2], second[2])
        one, two = jnp.exp2(first[2] - top), jnp.exp2(second[2] - top)
        return first[0] * one + second[0] * two, first[1] * one + second[1] * two, top

    shape = (half, ROWS, HD)
    place = lax.broadcasted_iota(jnp.int32, shape, 0)
    second_row = jnp.where(lax.broadcasted_iota(jnp.int32, shape, 1) < PER_GROUP, 0, 1)

    def with_slots(value, part, mine):
        at = place + x * y_chips + part * half
        at = jnp.where(at < chips, at, at - chips)
        answer = at * 4 + second_row + 2 * (core if mine else 1 - core)
        value = tuple(each.reshape(shape) for each in value)
        hits = [answer == sans[at] for at in range(2)]
        held = [[jnp.broadcast_to(slot[at, which][None], shape) for which in range(3)] for at in range(2)]
        piece = [jnp.where(hits[0], held[0][which], held[1][which]) for which in range(3)]
        piece[2] = jnp.where(hits[0], held[0][2], jnp.where(hits[1], held[1][2], NEG_BIG))
        return tuple(each.reshape(unit_rows, HD) for each in merged(value, piece))

    lane = lax.broadcasted_iota(jnp.int32, (unit_rows, HD), 1)

    def give_half(part, value):
        total_sum, total, top = with_slots(value, part, False)
        give[part, 0] = total_sum
        give[part, 1] = jnp.where(lane < 64, top, total)
        partials(part).start()

    def send_half(part, mine):
        mine = with_slots(mine, part, True)
        partials(part).wait_recv()
        stats = take[part, 1]
        theirs = (
            take[part, 0],
            jnp.broadcast_to(stats[:, 64:65], (unit_rows, HD)),
            jnp.broadcast_to(stats[:, 0:1], (unit_rows, HD)),
        )
        total_sum, total, top = merged(mine, theirs)
        high = total.astype(BF16).astype(F32)
        stats = jnp.where(lane < 32, top, jnp.where(lane < 64, high, total - high))
        blocks = pl.ds(part * half, half)
        msg[blocks, 0:ROWS, :] = total_sum.astype(BF16).reshape(shape)
        msg[blocks, ROWS : 2 * ROWS, :] = stats.astype(BF16).reshape(shape)
        for group in range(part * x_chips // 2, (part + 1) * x_chips // 2):
            column = (x + group) % x_chips * y_chips

            def send(yy, group=group, column=column):
                pltpu.make_async_remote_copy(
                    src_ref=msg.at[group * y_chips + yy],
                    dst_ref=got.at[(x_chips - group) % x_chips * y_chips + y],
                    send_sem=msend,
                    recv_sem=mrecv,
                    device_id=((column + yy) * 2 + core, z),
                    device_id_type=MESH,
                ).start()

            if group == 0:
                start_others(0, y_chips, y, send)
                got[y] = msg[y]
            else:
                pl.loop(0, y_chips)(send)

    for group in range(x_chips // 2):
        await_queries(group)
    forward(0).start()
    _, top = turn(None, None, 0, even)
    for group in range(x_chips // 2, x_chips):
        await_queries(group)
    forward(1).start()
    copies[1].wait()
    forward(0).wait_recv()
    own_first, top = turn(even, top, chips, odd)
    for which in range(3):
        own[which] = own_first[which]
    forward(1).wait_recv()
    copies[2].wait()
    copies[3].wait()
    for at in range(2):
        suffix(at)
    other, top = turn(odd, top, chips + half, even)
    give_half(0, other)
    other, top = turn(even, top, half, odd)
    give_half(1, other)
    send_half(0, tuple(own[which] for which in range(3)))
    own_second, _ = turn(odd, top, None, None)
    send_half(1, own_second)

    def whole(ref, count, send_sem, recv_sem):
        part = ref.at[pl.ds(0, count)]
        return pltpu.make_async_remote_copy(
            src_ref=part, dst_ref=part, send_sem=send_sem, recv_sem=recv_sem, device_id=(sibling, z), device_id_type=MESH
        )

    whole(got, chips - 1, msend, mrecv).wait_recv()
    sums = got[:, 0:ROWS, :].astype(F32)
    stats = got[:, ROWS : 2 * ROWS, :].astype(F32)
    tops = jnp.broadcast_to(stats[:, :, 0:1], sums.shape)
    totals = jnp.broadcast_to(stats[:, :, 32:33], sums.shape) + jnp.broadcast_to(stats[:, :, 64:65], sums.shape)
    factor = jnp.exp2(tops - jnp.max(tops, axis=0, keepdims=True))
    result = jnp.sum(sums * factor, axis=0) / jnp.sum(totals * factor, axis=0)
    zbuf[z] = result.astype(BF16)

    def send_result(to):
        pltpu.make_async_remote_copy(
            src_ref=zbuf.at[z], dst_ref=zbuf.at[z], send_sem=zsend, recv_sem=zrecv, device_id=(seq, to), device_id_type=MESH
        ).start()

    start_others(0, z_chips, z, send_result)

    whole(qbuf, chips - 1, qsend, mrecv).wait_send()
    for part in range(2):
        forward(part).wait_send()
        partials(part).wait_send()
    whole(msg, chips - 1, msend, mrecv).wait_send()
    heads = whole(zbuf, z_chips - 1, zsend, zrecv)
    heads.wait_recv()
    out_ref[...] = zbuf[...]
    heads.wait_send()


def on_device(x_chips, queries, prefix_keys, prefix_values, suffix_keys, suffix_values, suffix_length, slot_answer):
    z_chips = lax.axis_size("head")
    chips = lax.axis_size("seq") // 2
    y_chips = chips // x_chips
    keys, cap = prefix_keys.shape[0], suffix_keys.shape[1]
    unit_rows = chips // 2 * ROWS
    chunk = min(1024, keys)
    hbm = pl.BlockSpec(memory_space=pltpu.MemorySpace.HBM)
    vmem = pl.BlockSpec(memory_space=pltpu.VMEM)
    smem = pl.BlockSpec(memory_space=pltpu.SMEM)
    dma = pltpu.SemaphoreType.DMA
    heads = pl.pallas_call(
        functools.partial(attend, x_chips, y_chips, z_chips, chunk),
        out_shape=jax.ShapeDtypeStruct((z_chips, ROWS, HD), BF16),
        in_specs=[hbm, hbm, hbm, hbm, hbm, smem, smem],
        out_specs=vmem,
        scratch_shapes=[
            pltpu.VMEM((2, PER_GROUP * HD), BF16),
            pltpu.VMEM((ROWS, HD), BF16),
            pltpu.VMEM((2 * chips, ROWS, HD), BF16),
            pltpu.VMEM((keys, HD), BF16),
            pltpu.VMEM((HD, keys), BF16),
            pltpu.VMEM((keys, HD), BF16),
            pltpu.VMEM((2, cap, HD), BF16),
            pltpu.VMEM((2, cap, HD), BF16),
            pltpu.VMEM((unit_rows, keys), F32),
            pltpu.VMEM((unit_rows, keys), F32),
            pltpu.VMEM((3, unit_rows, HD), F32),
            pltpu.VMEM((2, 2, unit_rows, HD), F32),
            pltpu.VMEM((2, 2, unit_rows, HD), F32),
            pltpu.VMEM((2, 3, ROWS, HD), F32),
            pltpu.VMEM((chips, 2 * ROWS, HD), BF16),
            pltpu.VMEM((chips, 2 * ROWS, HD), BF16),
            pltpu.VMEM((z_chips, ROWS, HD), BF16),
            dma((5,)),
            dma,
            dma((x_chips,)),
            dma((2,)),
            dma((2,)),
            dma((2,)),
            dma((2,)),
            dma,
            dma,
            dma,
            dma,
        ],
        compiler_params=pltpu.CompilerParams(collective_id=0, has_side_effects=True, vmem_limit_bytes=60 << 20),
        name="attend",
    )(
        queries,
        prefix_keys,
        prefix_values,
        suffix_keys,
        suffix_values,
        suffix_length,
        slot_answer,
    )
    heads = heads.reshape(z_chips, 2, PER_GROUP * HD)
    return jnp.swapaxes(heads, 0, 1).reshape(2, z_chips * PER_GROUP * HD)


def solution(mesh):
    in_specs = (
        P("seq", "head"),
        P("seq", "head"),
        P("seq", "head"),
        P("seq", None, "head"),
        P("seq", None, "head"),
        P("seq"),
        P("seq"),
    )
    return jax.shard_map(
        functools.partial(on_device, 4), mesh=mesh, in_specs=in_specs, out_specs=P("seq", None), check_vma=False
    )
```

```python
import functools
import math

import jax
import jax.numpy as jnp
from jax import lax
from jax.experimental import pallas as pl
from jax.experimental.pallas import tpu as pltpu
from jax.sharding import PartitionSpec as P

HD = 128
PER_GROUP = 8
NEG_BIG = -1e30
EXP2_SCALE = math.log2(math.e) / math.sqrt(HD)
ROWS = 16
F32 = jnp.float32
BF16 = jnp.bfloat16
MESH = pl.DeviceIdType.MESH


def attend(x_chips, y_chips, z_chips, chunk, q_ref, pk, pv, sk, sv, slen, sans, out_ref, qraw, qown, qbuf, kraw, kt, vbuf, skb, svb,
           even, odd, own, give, take, slot, msg, got, zbuf, local_sem, qsend, qrecv, fsend, frecv, psend, precv, msend, mrecv, zsend, zrecv):
    seq, z = lax.axis_index("seq"), lax.axis_index("head")
    chip = seq // 2
    core = seq - chip * 2
    x = chip // y_chips
    y = chip - x * y_chips
    sibling = chip * 2 + 1 - core
    chips = x_chips * y_chips
    half = chips // 2
    unit_rows = half * ROWS
    keys = kraw.shape[0]

    def others(count, me, act):
        for step in range(1, count):
            act(lax.rem(me + step, count))

    copies = [
        pltpu.make_async_copy(pk, kraw, local_sem.at[0]),
        pltpu.make_async_copy(pv, vbuf, local_sem.at[1]),
        pltpu.make_async_copy(sk, skb, local_sem.at[2]),
        pltpu.make_async_copy(sv, svb, local_sem.at[3]),
    ]
    query_copy = pltpu.make_async_copy(q_ref, qraw, local_sem.at[4])
    query_copy.start()

    barrier = pltpu.get_barrier_semaphore()

    def greet(to):
        pl.semaphore_signal(barrier, inc=1, device_id=to, device_id_type=MESH)

    columns = [lax.rem(x + group, x_chips) * y_chips for group in range(x_chips)]
    others(z_chips, z, lambda at: greet((seq, at)))
    for group in range(1, x_chips):
        for yy in range(y_chips):
            greet(((columns[group] + yy) * 2 + core, z))
    others(y_chips, y, lambda at: greet(((columns[0] + at) * 2 + core, z)))
    greet((sibling, z))
    for copy in copies:
        copy.start()

    query_copy.wait()
    raw = qraw[...].astype(F32)
    pieces = [raw[at : at + 1, h * HD : (h + 1) * HD] for at in range(2) for h in range(PER_GROUP)]
    block = jnp.concatenate(pieces, axis=0).astype(BF16)
    qown[...] = block
    qbuf[y] = block
    pl.semaphore_wait(barrier, 1 + (chips - 1) + (z_chips - 1))

    for group in range(x_chips):
        column = columns[(x_chips - group) % x_chips]

        def send_queries(yy, group=group, column=column):
            pltpu.make_async_remote_copy(
                src_ref=qown,
                dst_ref=qbuf.at[group * y_chips + y],
                send_sem=qsend,
                recv_sem=qrecv.at[group],
                device_id=((column + yy) * 2 + core, z),
                device_id_type=MESH,
            ).start()

        if group == 0:
            others(y_chips, y, send_queries)
        else:
            for yy in range(y_chips):
                send_queries(yy)

    copies[0].wait()

    @pl.loop(0, keys // chunk)
    def _(step):
        at = pl.multiple_of(step * chunk, chunk)
        kt[:, pl.ds(at, chunk)] = kraw[pl.ds(at, chunk), :].T

    def await_queries(group):
        first = 1 if group == 0 else 0
        part = qbuf.at[pl.ds(group * y_chips, y_chips - first)]
        pltpu.make_async_remote_copy(
            src_ref=part, dst_ref=part, send_sem=qsend, recv_sem=qrecv.at[group], device_id=(sibling, z), device_id_type=MESH
        ).wait_recv()

    def forward(part):
        return pltpu.make_async_remote_copy(
            src_ref=qbuf.at[pl.ds(part * half, half)],
            dst_ref=qbuf.at[pl.ds(chips + part * half, half)],
            send_sem=fsend.at[part],
            recv_sem=frecv.at[part],
            device_id=(sibling, z),
            device_id_type=MESH,
        )

    def partials(part):
        return pltpu.make_async_remote_copy(
            src_ref=give.at[part],
            dst_ref=take.at[part],
            send_sem=psend.at[part],
            recv_sem=precv.at[part],
            device_id=(sibling, z),
            device_id_type=MESH,
        )

    def stabiliser(scores_top):
        top = jnp.max(scores_top, axis=1, keepdims=True) * EXP2_SCALE
        return top.astype(BF16).astype(F32)

    def lane_tiles_max(scores):
        tiles = [scores[:, at : at + 128] for at in range(0, scores.shape[1], 128)]
        return functools.reduce(jnp.maximum, tiles)

    def weighted(scores, top, values):
        weights = jnp.exp2(scores * EXP2_SCALE - top).astype(BF16)
        wide = jnp.concatenate([values, jnp.ones(values.shape, BF16)], axis=1)
        return jnp.dot(weights, wide, preferred_element_type=F32)

    def turn(now, top, begin, later, midway=None):
        both, later_top = None, None
        rows = None if begin is None else qbuf[begin : begin + half].reshape(unit_rows, HD)
        for at in range(0, keys, chunk):
            if midway is not None and at == keys // 2:
                midway()
            if begin is not None:
                scores = jnp.dot(rows, kt[:, at : at + chunk], preferred_element_type=F32)
                later[:, at : at + chunk] = scores
                here = lane_tiles_max(scores)
                later_top = here if later_top is None else jnp.maximum(later_top, here)
            if now is not None:
                here = weighted(now[:, at : at + chunk], top, vbuf[at : at + chunk, :])
                both = here if both is None else both + here
        part = None if now is None else (both[:, :HD], both[:, HD:], jnp.broadcast_to(top, (unit_rows, HD)))
        return part, None if begin is None else stabiliser(later_top)

    def suffix(at):
        holder = sans[at] // 2
        block = (holder + core) % 2 * chips + (holder // 2 - x * y_chips + chips) % chips
        scores = lax.dot_general(qbuf[block], skb[at], (((1,), (1,)), ((), ())), preferred_element_type=F32)
        position = lax.broadcasted_iota(jnp.int32, scores.shape, 1)
        scores = jnp.where(position < slen[at], scores, NEG_BIG)
        top = stabiliser(lane_tiles_max(scores))
        both = weighted(scores, top, svb[at])
        slot[at, 0] = both[:, :HD]
        slot[at, 1] = both[:, HD:]
        slot[at, 2] = jnp.broadcast_to(top, (ROWS, HD))

    def merged(first, second):
        top = jnp.maximum(first[2], second[2])
        one, two = jnp.exp2(first[2] - top), jnp.exp2(second[2] - top)
        return first[0] * one + second[0] * two, first[1] * one + second[1] * two, top

    shape = (half, ROWS, HD)
    place = lax.broadcasted_iota(jnp.int32, shape, 0)
    second_row = jnp.where(lax.broadcasted_iota(jnp.int32, shape, 1) < PER_GROUP, 0, 1)

    def with_slots(value, part, mine):
        at = place + x * y_chips + part * half
        at = jnp.where(at < chips, at, at - chips)
        answer = at * 4 + second_row + 2 * (core if mine else 1 - core)
        value = tuple(each.reshape(shape) for each in value)
        hits = [answer == sans[at] for at in range(2)]
        held = [[jnp.broadcast_to(slot[at, which][None], shape) for which in range(3)] for at in range(2)]
        piece = [jnp.where(hits[0], held[0][which], held[1][which]) for which in range(3)]
        piece[2] = jnp.where(hits[0], held[0][2], jnp.where(hits[1], held[1][2], NEG_BIG))
        return tuple(each.reshape(unit_rows, HD) for each in merged(value, piece))

    lane = lax.broadcasted_iota(jnp.int32, (unit_rows, HD), 1)

    def give_half(part, value):
        total_sum, total, top = with_slots(value, part, False)
        give[part, 0] = total_sum
        give[part, 1] = jnp.where(lane < 64, top, total)
        partials(part).start()

    def send_half(part, mine):
        mine = with_slots(mine, part, True)
        partials(part).wait_recv()
        stats = take[part, 1]
        theirs = (
            take[part, 0],
            jnp.broadcast_to(stats[:, 64:65], (unit_rows, HD)),
            jnp.broadcast_to(stats[:, 0:1], (unit_rows, HD)),
        )
        total_sum, total, top = merged(mine, theirs)
        high = total.astype(BF16).astype(F32)
        stats = jnp.where(lane < 32, top, jnp.where(lane < 64, high, total - high))
        blocks = pl.ds(part * half, half)
        msg[blocks, 0:ROWS, :] = total_sum.astype(BF16).reshape(shape)
        msg[blocks, ROWS : 2 * ROWS, :] = stats.astype(BF16).reshape(shape)
        for group in range(part * x_chips // 2, (part + 1) * x_chips // 2):
            column = columns[group]

            def send(yy, group=group, column=column):
                pltpu.make_async_remote_copy(
                    src_ref=msg.at[group * y_chips + yy],
                    dst_ref=got.at[(x_chips - group) % x_chips * y_chips + y],
                    send_sem=msend,
                    recv_sem=mrecv,
                    device_id=((column + yy) * 2 + core, z),
                    device_id_type=MESH,
                ).start()

            if group == 0:
                others(y_chips, y, send)
                got[y] = msg[y]
            else:
                for yy in range(y_chips):
                    send(yy)

    for group in range(x_chips // 2):
        await_queries(group)
    forward(0).start()
    _, top = turn(None, None, 0, even)
    for group in range(x_chips // 2, x_chips):
        await_queries(group)
    forward(1).start()
    copies[1].wait()
    forward(0).wait_recv()
    own_first, top = turn(even, top, chips, odd)
    for which in range(3):
        own[which] = own_first[which]
    forward(1).wait_recv()
    copies[2].wait()
    copies[3].wait()
    for at in range(2):
        suffix(at)
    other, top = turn(odd, top, chips + half, even)
    give_half(0, other)
    other, top = turn(even, top, half, odd, lambda: send_half(0, tuple(own[which] for which in range(3))))
    give_half(1, other)
    own_second, _ = turn(odd, top, None, None)
    send_half(1, own_second)

    def whole(ref, count, send_sem, recv_sem):
        part = ref.at[pl.ds(0, count)]
        return pltpu.make_async_remote_copy(
            src_ref=part, dst_ref=part, send_sem=send_sem, recv_sem=recv_sem, device_id=(sibling, z), device_id_type=MESH
        )

    whole(got, chips - 1, msend, mrecv).wait_recv()
    sums = got[:, 0:ROWS, :].astype(F32)
    stats = got[:, ROWS : 2 * ROWS, :].astype(F32)
    tops = jnp.broadcast_to(stats[:, :, 0:1], sums.shape)
    totals = jnp.broadcast_to(stats[:, :, 32:33], sums.shape) + jnp.broadcast_to(stats[:, :, 64:65], sums.shape)
    factor = jnp.exp2(tops - jnp.max(tops, axis=0, keepdims=True))
    result = jnp.sum(sums * factor, axis=0) / jnp.sum(totals * factor, axis=0)
    wide = [jnp.concatenate([result[at * PER_GROUP + h][None] for h in range(PER_GROUP)], axis=1) for at in range(2)]
    zbuf[z] = jnp.concatenate(wide, axis=0).astype(BF16)

    def send_result(to):
        pltpu.make_async_remote_copy(
            src_ref=zbuf.at[z], dst_ref=zbuf.at[z], send_sem=zsend, recv_sem=zrecv, device_id=(seq, to), device_id_type=MESH
        ).start()

    others(z_chips, z, send_result)

    whole(qbuf, chips - 1, qsend, mrecv).wait_send()
    for part in range(2):
        forward(part).wait_send()
        partials(part).wait_send()
    whole(msg, chips - 1, msend, mrecv).wait_send()
    heads = whole(zbuf, z_chips - 1, zsend, zrecv)
    heads.wait_recv()
    out_ref[...] = zbuf[...]
    heads.wait_send()


def on_device(x_chips, queries, prefix_keys, prefix_values, suffix_keys, suffix_values, suffix_length, slot_answer):
    z_chips = lax.axis_size("head")
    chips = lax.axis_size("seq") // 2
    y_chips = chips // x_chips
    keys, cap = prefix_keys.shape[0], suffix_keys.shape[1]
    unit_rows = chips // 2 * ROWS
    chunk = min(1024, keys)
    hbm = pl.BlockSpec(memory_space=pltpu.MemorySpace.HBM)
    vmem = pl.BlockSpec(memory_space=pltpu.VMEM)
    smem = pl.BlockSpec(memory_space=pltpu.SMEM)
    dma = pltpu.SemaphoreType.DMA
    heads = pl.pallas_call(
        functools.partial(attend, x_chips, y_chips, z_chips, chunk),
        out_shape=jax.ShapeDtypeStruct((z_chips, 2, PER_GROUP * HD), BF16),
        in_specs=[hbm, hbm, hbm, hbm, hbm, smem, smem],
        out_specs=vmem,
        scratch_shapes=[
            pltpu.VMEM((2, PER_GROUP * HD), BF16),
            pltpu.VMEM((ROWS, HD), BF16),
            pltpu.VMEM((2 * chips, ROWS, HD), BF16),
            pltpu.VMEM((keys, HD), BF16),
            pltpu.VMEM((HD, keys), BF16),
            pltpu.VMEM((keys, HD), BF16),
            pltpu.VMEM((2, cap, HD), BF16),
            pltpu.VMEM((2, cap, HD), BF16),
            pltpu.VMEM((unit_rows, keys), F32),
            pltpu.VMEM((unit_rows, keys), F32),
            pltpu.VMEM((3, unit_rows, HD), F32),
            pltpu.VMEM((2, 2, unit_rows, HD), F32),
            pltpu.VMEM((2, 2, unit_rows, HD), F32),
            pltpu.VMEM((2, 3, ROWS, HD), F32),
            pltpu.VMEM((chips, 2 * ROWS, HD), BF16),
            pltpu.VMEM((chips, 2 * ROWS, HD), BF16),
            pltpu.VMEM((z_chips, 2, PER_GROUP * HD), BF16),
            dma((5,)),
            dma,
            dma((x_chips,)),
            dma((2,)),
            dma((2,)),
            dma((2,)),
            dma((2,)),
            dma,
            dma,
            dma,
            dma,
        ],
        compiler_params=pltpu.CompilerParams(collective_id=0, has_side_effects=True, vmem_limit_bytes=60 << 20),
        name="attend",
    )(
        queries,
        prefix_keys,
        prefix_values,
        suffix_keys,
        suffix_values,
        suffix_length,
        slot_answer,
    )
    return jnp.swapaxes(heads, 0, 1).reshape(2, z_chips * PER_GROUP * HD)


def solution(mesh):
    in_specs = (
        P("seq", "head"),
        P("seq", "head"),
        P("seq", "head"),
        P("seq", None, "head"),
        P("seq", None, "head"),
        P("seq"),
        P("seq"),
    )
    return jax.shard_map(
        functools.partial(on_device, 4), mesh=mesh, in_specs=in_specs, out_specs=P("seq", None), check_vma=False
    )
```

```python
import functools
import math

import jax
import jax.numpy as jnp
from jax import lax
from jax.experimental import pallas as pl
from jax.experimental.pallas import tpu as pltpu
from jax.sharding import PartitionSpec as P

HD = 128
PER_GROUP = 8
NEG_BIG = -1e30
EXP2_SCALE = math.log2(math.e) / math.sqrt(HD)
ROWS = 16
F32 = jnp.float32
BF16 = jnp.bfloat16
MESH = pl.DeviceIdType.MESH


def attend(x_chips, y_chips, z_chips, chunk, q_ref, pk, pv, sk, sv, slen, sans, out_ref, qraw, qown, qbuf, keys_here, vbuf, skb, svb,
           even, odd, own, give, take, slot, msg, got, zbuf, local_sem, qsend, qrecv, fsend, frecv, psend, precv, msend, mrecv, zsend, zrecv):
    seq, z = lax.axis_index("seq"), lax.axis_index("head")
    chip = seq // 2
    core = seq - chip * 2
    x = chip // y_chips
    y = chip - x * y_chips
    sibling = chip * 2 + 1 - core
    chips = x_chips * y_chips
    half = chips // 2
    unit_rows = half * ROWS
    keys = keys_here.shape[0]

    def others(count, me, act):
        for step in range(1, count):
            act(lax.rem(me + step, count))

    copies = [
        pltpu.make_async_copy(pk, keys_here, local_sem.at[0]),
        pltpu.make_async_copy(pv, vbuf, local_sem.at[1]),
        pltpu.make_async_copy(sk, skb, local_sem.at[2]),
        pltpu.make_async_copy(sv, svb, local_sem.at[3]),
    ]
    query_copy = pltpu.make_async_copy(q_ref, qraw, local_sem.at[4])
    query_copy.start()

    barrier = pltpu.get_barrier_semaphore()

    def greet(to):
        pl.semaphore_signal(barrier, inc=1, device_id=to, device_id_type=MESH)

    columns = [lax.rem(x + group, x_chips) * y_chips for group in range(x_chips)]
    others(z_chips, z, lambda at: greet((seq, at)))
    for group in range(1, x_chips):
        for yy in range(y_chips):
            greet(((columns[group] + yy) * 2 + core, z))
    others(y_chips, y, lambda at: greet(((columns[0] + at) * 2 + core, z)))
    greet((sibling, z))
    for copy in copies:
        copy.start()

    query_copy.wait()
    raw = qraw[...].astype(F32)
    pieces = [raw[at : at + 1, h * HD : (h + 1) * HD] for at in range(2) for h in range(PER_GROUP)]
    block = jnp.concatenate(pieces, axis=0).astype(BF16)
    qown[...] = block
    qbuf[y] = block
    pl.semaphore_wait(barrier, 1 + (chips - 1) + (z_chips - 1))

    for group in range(x_chips):
        column = columns[(x_chips - group) % x_chips]

        def send_queries(yy, group=group, column=column):
            pltpu.make_async_remote_copy(
                src_ref=qown,
                dst_ref=qbuf.at[group * y_chips + y],
                send_sem=qsend,
                recv_sem=qrecv.at[group],
                device_id=((column + yy) * 2 + core, z),
                device_id_type=MESH,
            ).start()

        if group == 0:
            others(y_chips, y, send_queries)
        else:
            for yy in range(y_chips):
                send_queries(yy)

    copies[0].wait()

    def await_queries(group):
        first = 1 if group == 0 else 0
        part = qbuf.at[pl.ds(group * y_chips, y_chips - first)]
        pltpu.make_async_remote_copy(
            src_ref=part, dst_ref=part, send_sem=qsend, recv_sem=qrecv.at[group], device_id=(sibling, z), device_id_type=MESH
        ).wait_recv()

    def forward(part):
        return pltpu.make_async_remote_copy(
            src_ref=qbuf.at[pl.ds(part * half, half)],
            dst_ref=qbuf.at[pl.ds(chips + part * half, half)],
            send_sem=fsend.at[part],
            recv_sem=frecv.at[part],
            device_id=(sibling, z),
            device_id_type=MESH,
        )

    def partials(part):
        return pltpu.make_async_remote_copy(
            src_ref=give.at[part],
            dst_ref=take.at[part],
            send_sem=psend.at[part],
            recv_sem=precv.at[part],
            device_id=(sibling, z),
            device_id_type=MESH,
        )

    def stabiliser(scores_top):
        top = jnp.max(scores_top, axis=1, keepdims=True) * EXP2_SCALE
        return top.astype(BF16).astype(F32)

    def lane_tiles_max(scores):
        tiles = [scores[:, at : at + 128] for at in range(0, scores.shape[1], 128)]
        return functools.reduce(jnp.maximum, tiles)

    def weighted(scores, top, values):
        weights = jnp.exp2(scores * EXP2_SCALE - top).astype(BF16)
        wide = jnp.concatenate([values, jnp.ones(values.shape, BF16)], axis=1)
        return jnp.dot(weights, wide, preferred_element_type=F32)

    def inner(rows, columns):
        return lax.dot_general(rows, columns, (((1,), (1,)), ((), ())), preferred_element_type=F32)

    def turn(now, top, begin, later, midway=None):
        both, later_top = None, None
        rows = None if begin is None else qbuf[begin : begin + half].reshape(unit_rows, HD)
        for at in range(0, keys, chunk):
            if midway is not None and at == keys // 2:
                midway()
            if begin is not None:
                scores = inner(rows, keys_here[at : at + chunk, :])
                later[:, at : at + chunk] = scores
                here = lane_tiles_max(scores)
                later_top = here if later_top is None else jnp.maximum(later_top, here)
            if now is not None:
                here = weighted(now[:, at : at + chunk], top, vbuf[at : at + chunk, :])
                both = here if both is None else both + here
        part = None if now is None else (both[:, :HD], both[:, HD:], jnp.broadcast_to(top, (unit_rows, HD)))
        return part, None if begin is None else stabiliser(later_top)

    def suffix(at):
        holder = sans[at] // 2
        block = (holder + core) % 2 * chips + (holder // 2 - x * y_chips + chips) % chips
        scores = inner(qbuf[block], skb[at])
        position = lax.broadcasted_iota(jnp.int32, scores.shape, 1)
        scores = jnp.where(position < slen[at], scores, NEG_BIG)
        top = stabiliser(lane_tiles_max(scores))
        both = weighted(scores, top, svb[at])
        slot[at, 0] = both[:, :HD]
        slot[at, 1] = both[:, HD:]
        slot[at, 2] = jnp.broadcast_to(top, (ROWS, HD))

    def merged(first, second):
        top = jnp.maximum(first[2], second[2])
        one, two = jnp.exp2(first[2] - top), jnp.exp2(second[2] - top)
        return first[0] * one + second[0] * two, first[1] * one + second[1] * two, top

    shape = (half, ROWS, HD)
    place = lax.broadcasted_iota(jnp.int32, shape, 0)
    second_row = jnp.where(lax.broadcasted_iota(jnp.int32, shape, 1) < PER_GROUP, 0, 1)

    def with_slots(value, part, mine):
        at = place + x * y_chips + part * half
        at = jnp.where(at < chips, at, at - chips)
        answer = at * 4 + second_row + 2 * (core if mine else 1 - core)
        value = tuple(each.reshape(shape) for each in value)
        hits = [answer == sans[at] for at in range(2)]
        held = [[jnp.broadcast_to(slot[at, which][None], shape) for which in range(3)] for at in range(2)]
        piece = [jnp.where(hits[0], held[0][which], held[1][which]) for which in range(3)]
        piece[2] = jnp.where(hits[0], held[0][2], jnp.where(hits[1], held[1][2], NEG_BIG))
        return tuple(each.reshape(unit_rows, HD) for each in merged(value, piece))

    lane = lax.broadcasted_iota(jnp.int32, (unit_rows, HD), 1)

    def give_half(part, value):
        total_sum, total, top = with_slots(value, part, False)
        give[part, 0] = total_sum
        give[part, 1] = jnp.where(lane < 64, top, total)
        partials(part).start()

    def send_half(part, mine):
        mine = with_slots(mine, part, True)
        partials(part).wait_recv()
        stats = take[part, 1]
        theirs = (
            take[part, 0],
            jnp.broadcast_to(stats[:, 64:65], (unit_rows, HD)),
            jnp.broadcast_to(stats[:, 0:1], (unit_rows, HD)),
        )
        total_sum, total, top = merged(mine, theirs)
        high = total.astype(BF16).astype(F32)
        stats = jnp.where(lane < 32, top, jnp.where(lane < 64, high, total - high))
        blocks = pl.ds(part * half, half)
        msg[blocks, 0:ROWS, :] = total_sum.astype(BF16).reshape(shape)
        msg[blocks, ROWS : 2 * ROWS, :] = stats.astype(BF16).reshape(shape)
        for group in range(part * x_chips // 2, (part + 1) * x_chips // 2):
            column = columns[group]

            def send(yy, group=group, column=column):
                pltpu.make_async_remote_copy(
                    src_ref=msg.at[group * y_chips + yy],
                    dst_ref=got.at[(x_chips - group) % x_chips * y_chips + y],
                    send_sem=msend,
                    recv_sem=mrecv,
                    device_id=((column + yy) * 2 + core, z),
                    device_id_type=MESH,
                ).start()

            if group == 0:
                others(y_chips, y, send)
                got[y] = msg[y]
            else:
                for yy in range(y_chips):
                    send(yy)

    for group in range(x_chips // 2):
        await_queries(group)
    forward(0).start()
    _, top = turn(None, None, 0, even)
    for group in range(x_chips // 2, x_chips):
        await_queries(group)
    forward(1).start()
    copies[1].wait()
    forward(0).wait_recv()
    own_first, top = turn(even, top, chips, odd)
    for which in range(3):
        own[which] = own_first[which]
    forward(1).wait_recv()
    copies[2].wait()
    copies[3].wait()
    for at in range(2):
        suffix(at)
    other, top = turn(odd, top, chips + half, even)
    give_half(0, other)
    other, top = turn(even, top, half, odd, lambda: send_half(0, tuple(own[which] for which in range(3))))
    give_half(1, other)
    own_second, _ = turn(odd, top, None, None)
    send_half(1, own_second)

    def whole(ref, count, send_sem, recv_sem):
        part = ref.at[pl.ds(0, count)]
        return pltpu.make_async_remote_copy(
            src_ref=part, dst_ref=part, send_sem=send_sem, recv_sem=recv_sem, device_id=(sibling, z), device_id_type=MESH
        )

    whole(got, chips - 1, msend, mrecv).wait_recv()
    sums = got[:, 0:ROWS, :].astype(F32)
    stats = got[:, ROWS : 2 * ROWS, :].astype(F32)
    tops = jnp.broadcast_to(stats[:, :, 0:1], sums.shape)
    totals = jnp.broadcast_to(stats[:, :, 32:33], sums.shape) + jnp.broadcast_to(stats[:, :, 64:65], sums.shape)
    factor = jnp.exp2(tops - jnp.max(tops, axis=0, keepdims=True))
    result = jnp.sum(sums * factor, axis=0) / jnp.sum(totals * factor, axis=0)
    wide = [jnp.concatenate([result[at * PER_GROUP + h][None] for h in range(PER_GROUP)], axis=1) for at in range(2)]
    zbuf[z] = jnp.concatenate(wide, axis=0).astype(BF16)

    def send_result(to):
        pltpu.make_async_remote_copy(
            src_ref=zbuf.at[z], dst_ref=zbuf.at[z], send_sem=zsend, recv_sem=zrecv, device_id=(seq, to), device_id_type=MESH
        ).start()

    others(z_chips, z, send_result)

    whole(qbuf, chips - 1, qsend, mrecv).wait_send()
    for part in range(2):
        forward(part).wait_send()
        partials(part).wait_send()
    whole(msg, chips - 1, msend, mrecv).wait_send()
    heads = whole(zbuf, z_chips - 1, zsend, zrecv)
    heads.wait_recv()
    out_ref[...] = zbuf[...]
    heads.wait_send()


def on_device(x_chips, *arrays):
    _, prefix_keys, _, suffix_keys, _, _, _ = arrays
    z_chips = lax.axis_size("head")
    chips = lax.axis_size("seq") // 2
    y_chips = chips // x_chips
    keys, cap = prefix_keys.shape[0], suffix_keys.shape[1]
    unit_rows = chips // 2 * ROWS
    chunk = min(1024, keys)
    hbm = pl.BlockSpec(memory_space=pltpu.MemorySpace.HBM)
    vmem = pl.BlockSpec(memory_space=pltpu.VMEM)
    smem = pl.BlockSpec(memory_space=pltpu.SMEM)
    dma = pltpu.SemaphoreType.DMA
    heads = pl.pallas_call(
        functools.partial(attend, x_chips, y_chips, z_chips, chunk),
        out_shape=pltpu.VMEM((z_chips, 2, PER_GROUP * HD), BF16),
        in_specs=[hbm, hbm, hbm, hbm, hbm, smem, smem],
        out_specs=vmem,
        scratch_shapes=[
            pltpu.VMEM((2, PER_GROUP * HD), BF16),
            pltpu.VMEM((ROWS, HD), BF16),
            pltpu.VMEM((2 * chips, ROWS, HD), BF16),
            pltpu.VMEM((keys, HD), BF16),
            pltpu.VMEM((keys, HD), BF16),
            pltpu.VMEM((2, cap, HD), BF16),
            pltpu.VMEM((2, cap, HD), BF16),
            pltpu.VMEM((unit_rows, keys), F32),
            pltpu.VMEM((unit_rows, keys), F32),
            pltpu.VMEM((3, unit_rows, HD), F32),
            pltpu.VMEM((2, 2, unit_rows, HD), F32),
            pltpu.VMEM((2, 2, unit_rows, HD), F32),
            pltpu.VMEM((2, 3, ROWS, HD), F32),
            pltpu.VMEM((chips, 2 * ROWS, HD), BF16),
            pltpu.VMEM((chips, 2 * ROWS, HD), BF16),
            pltpu.VMEM((z_chips, 2, PER_GROUP * HD), BF16),
            dma((5,)),
            dma,
            dma((x_chips,)),
            dma((2,)),
            dma((2,)),
            dma((2,)),
            dma((2,)),
            dma,
            dma,
            dma,
            dma,
        ],
        compiler_params=pltpu.CompilerParams(collective_id=0, has_side_effects=True, vmem_limit_bytes=56 << 20),
        name="attend",
    )(
        *(pltpu.with_memory_space_constraint(each, pltpu.MemorySpace.HBM) for each in arrays)
    )
    return jnp.swapaxes(heads, 0, 1).reshape(2, z_chips * PER_GROUP * HD)


def solution(mesh):
    in_specs = (
        P("seq", "head"),
        P("seq", "head"),
        P("seq", "head"),
        P("seq", None, "head"),
        P("seq", None, "head"),
        P("seq"),
        P("seq"),
    )
    return jax.shard_map(
        functools.partial(on_device, 4), mesh=mesh, in_specs=in_specs, out_specs=P("seq", None), check_vma=False
    )
```

```python
import functools
import math

import jax
import jax.numpy as jnp
from jax import lax
from jax.experimental import pallas as pl
from jax.experimental.pallas import tpu as pltpu
from jax.sharding import PartitionSpec as P

HD = 128
PER_GROUP = 8
NEG_BIG = -1e30
EXP2_SCALE = math.log2(math.e) / math.sqrt(HD)
ROWS = 16
F32 = jnp.float32
BF16 = jnp.bfloat16
MESH = pl.DeviceIdType.MESH


def attend(x_chips, y_chips, z_chips, chunk, q_ref, pk, pv, sk, sv, slen, sans, out_ref, qraw, qown, qbuf, keys_here, vbuf, skb, svb,
           even, odd, own, give, take, slot, msg, got, stat, gotstat, zbuf, local_sem, qsend, qrecv, fsend, frecv, psend, precv, msend, mrecv,
           ssend, srecv, zsend, zrecv):
    seq, z = lax.axis_index("seq"), lax.axis_index("head")
    chip = seq // 2
    core = seq - chip * 2
    x = chip // y_chips
    y = chip - x * y_chips
    sibling = chip * 2 + 1 - core
    chips = x_chips * y_chips
    half = chips // 2
    unit_rows = half * ROWS
    keys = keys_here.shape[0]

    def others(count, me, act):
        for step in range(1, count):
            act(lax.rem(me + step, count))

    copies = [
        pltpu.make_async_copy(pk, keys_here, local_sem.at[0]),
        pltpu.make_async_copy(pv, vbuf, local_sem.at[1]),
        pltpu.make_async_copy(sk, skb, local_sem.at[2]),
        pltpu.make_async_copy(sv, svb, local_sem.at[3]),
    ]
    query_copy = pltpu.make_async_copy(q_ref, qraw, local_sem.at[4])
    query_copy.start()

    barrier = pltpu.get_barrier_semaphore()

    def greet(to):
        pl.semaphore_signal(barrier, inc=1, device_id=to, device_id_type=MESH)

    columns = [lax.rem(x + group, x_chips) * y_chips for group in range(x_chips)]
    others(z_chips, z, lambda at: greet((seq, at)))
    for group in range(1, x_chips):
        for yy in range(y_chips):
            greet(((columns[group] + yy) * 2 + core, z))
    others(y_chips, y, lambda at: greet(((columns[0] + at) * 2 + core, z)))
    greet((sibling, z))
    for copy in copies:
        copy.start()

    query_copy.wait()
    raw = qraw[...].astype(F32)
    pieces = [raw[at : at + 1, h * HD : (h + 1) * HD] for at in range(2) for h in range(PER_GROUP)]
    block = jnp.concatenate(pieces, axis=0).astype(BF16)
    qown[...] = block
    qbuf[y] = block
    pl.semaphore_wait(barrier, 1 + (chips - 1) + (z_chips - 1))

    for group in range(x_chips):
        column = columns[(x_chips - group) % x_chips]

        def send_queries(yy, group=group, column=column):
            pltpu.make_async_remote_copy(
                src_ref=qown,
                dst_ref=qbuf.at[group * y_chips + y],
                send_sem=qsend,
                recv_sem=qrecv.at[group],
                device_id=((column + yy) * 2 + core, z),
                device_id_type=MESH,
            ).start()

        if group == 0:
            others(y_chips, y, send_queries)
        else:
            for yy in range(y_chips):
                send_queries(yy)

    copies[0].wait()

    def await_queries(group):
        first = 1 if group == 0 else 0
        part = qbuf.at[pl.ds(group * y_chips, y_chips - first)]
        pltpu.make_async_remote_copy(
            src_ref=part, dst_ref=part, send_sem=qsend, recv_sem=qrecv.at[group], device_id=(sibling, z), device_id_type=MESH
        ).wait_recv()

    def forward(group):
        return pltpu.make_async_remote_copy(
            src_ref=qbuf.at[pl.ds(group * y_chips, y_chips)],
            dst_ref=qbuf.at[pl.ds(chips + group * y_chips, y_chips)],
            send_sem=fsend.at[group],
            recv_sem=frecv.at[group],
            device_id=(sibling, z),
            device_id_type=MESH,
        )

    def partials(part):
        return pltpu.make_async_remote_copy(
            src_ref=give.at[part],
            dst_ref=take.at[part],
            send_sem=psend.at[part],
            recv_sem=precv.at[part],
            device_id=(sibling, z),
            device_id_type=MESH,
        )

    def stabiliser(scores_top):
        top = jnp.max(scores_top, axis=1, keepdims=True) * EXP2_SCALE
        return top.astype(BF16).astype(F32)

    def lane_tiles_max(scores):
        tiles = [scores[:, at : at + 128] for at in range(0, scores.shape[1], 128)]
        return functools.reduce(jnp.maximum, tiles)

    def weighted(scores, top, values):
        weights = jnp.exp2(scores * EXP2_SCALE - top).astype(BF16)
        wide = jnp.concatenate([values, jnp.ones(values.shape, BF16)], axis=1)
        return jnp.dot(weights, wide, preferred_element_type=F32)

    def inner(rows, columns):
        return lax.dot_general(rows, columns, (((1,), (1,)), ((), ())), preferred_element_type=F32)

    def turn(now, top, begin, later, midway=None, piece=None):
        both, later_top = None, None
        span = slice(0, unit_rows) if piece is None else piece
        size = span.stop - span.start
        rows = None if begin is None else qbuf[begin : begin + size // ROWS].reshape(size, HD)
        for at in range(0, keys, chunk):
            if midway is not None and at == keys // 2:
                midway()
            if begin is not None:
                scores = inner(rows, keys_here[at : at + chunk, :])
                later[span, at : at + chunk] = scores
                here = lane_tiles_max(scores)
                later_top = here if later_top is None else jnp.maximum(later_top, here)
            if now is not None:
                here = weighted(now[span, at : at + chunk], top, vbuf[at : at + chunk, :])
                both = here if both is None else both + here
        part = None if now is None else (both[:, :HD], both[:, HD:], jnp.broadcast_to(top, (size, HD)))
        return part, None if begin is None else stabiliser(later_top)

    def suffix(at):
        holder = sans[at] // 2
        block = (holder + core) % 2 * chips + (holder // 2 - x * y_chips + chips) % chips
        scores = inner(qbuf[block], skb[at])
        position = lax.broadcasted_iota(jnp.int32, scores.shape, 1)
        scores = jnp.where(position < slen[at], scores, NEG_BIG)
        top = stabiliser(lane_tiles_max(scores))
        both = weighted(scores, top, svb[at])
        slot[at, 0] = both[:, :HD]
        slot[at, 1] = both[:, HD:]
        slot[at, 2] = jnp.broadcast_to(top, (ROWS, HD))

    def merged(first, second):
        top = jnp.maximum(first[2], second[2])
        one, two = jnp.exp2(first[2] - top), jnp.exp2(second[2] - top)
        return first[0] * one + second[0] * two, first[1] * one + second[1] * two, top

    def with_slots(value, first, mine):
        size = value[0].shape[0]
        shape = (size // ROWS, ROWS, HD)
        place = lax.broadcasted_iota(jnp.int32, shape, 0)
        second_row = jnp.where(lax.broadcasted_iota(jnp.int32, shape, 1) < PER_GROUP, 0, 1)
        at = place + (x * y_chips + first)
        at = jnp.where(at < chips, at, at - chips)
        answer = at * 4 + second_row + 2 * (core if mine else 1 - core)
        value = tuple(each.reshape(shape) for each in value)
        hits = [answer == sans[at] for at in range(2)]
        held = [[jnp.broadcast_to(slot[at, which][None], shape) for which in range(3)] for at in range(2)]
        piece = [jnp.where(hits[0], held[0][which], held[1][which]) for which in range(3)]
        piece[2] = jnp.where(hits[0], held[0][2], jnp.where(hits[1], held[1][2], NEG_BIG))
        return tuple(each.reshape(size, HD) for each in merged(value, piece))

    def give_half(part, value):
        total_sum, total, top = with_slots(value, part * half, False)
        lane = lax.broadcasted_iota(jnp.int32, total.shape, 1)
        give[part, 0] = total_sum
        give[part, 1] = jnp.where(lane < 64, top, total)
        partials(part).start()

    def diagonal(shape, begin):
        return lax.broadcasted_iota(jnp.int32, shape, 2) == lax.broadcasted_iota(jnp.int32, shape, 1) + begin

    def send_groups(groups, mine):
        first, size = groups[0] * y_chips, len(groups) * y_chips * ROWS
        part = first // half
        mine = with_slots(mine, first, True)
        span = slice((first - part * half) * ROWS, (first - part * half) * ROWS + size)
        stats = take[part, 1, span]
        theirs = (
            take[part, 0, span],
            jnp.broadcast_to(stats[:, 64:65], (size, HD)),
            jnp.broadcast_to(stats[:, 0:1], (size, HD)),
        )
        shape = (size // ROWS, ROWS, HD)
        total_sum, total, top = (each.reshape(shape) for each in merged(mine, theirs))
        blocks = slice(first, first + size // ROWS)
        msg[blocks] = total_sum.astype(BF16)
        row = jnp.where(diagonal(shape, 0), top, jnp.where(diagonal(shape, ROWS), total, 0.0))
        stat[blocks] = jnp.sum(row, axis=1, keepdims=True)
        for group in groups:

            def send(yy, group=group):
                to = ((columns[group] + yy) * 2 + core, z)
                for source, target, send_sem, recv_sem in ((msg, got, msend, mrecv), (stat, gotstat, ssend, srecv)):
                    pltpu.make_async_remote_copy(
                        src_ref=source.at[group * y_chips + yy],
                        dst_ref=target.at[group * y_chips + y],
                        send_sem=send_sem,
                        recv_sem=recv_sem.at[part],
                        device_id=to,
                        device_id_type=MESH,
                    ).start()

            if group == 0:
                others(y_chips, y, send)
                got[y] = msg[y]
                gotstat[y] = stat[y]
            else:
                for yy in range(y_chips):
                    send(yy)

    group_rows = y_chips * ROWS
    pieces = [slice(at, at + group_rows) for at in range(0, unit_rows, group_rows)]
    tops = []
    for group, piece in enumerate(pieces):
        await_queries(group)
        forward(group).start()
        tops.append(turn(None, None, group * y_chips, even, piece=piece)[1])
    top = jnp.concatenate(tops, axis=0)
    for group in range(x_chips // 2, x_chips):
        await_queries(group)
        forward(group).start()
    copies[1].wait()
    for group in range(x_chips // 2):
        forward(group).wait_recv()
    own_first, top = turn(even, top, chips, odd)
    for which in range(3):
        own[which] = own_first[which]
    for group in range(x_chips // 2, x_chips):
        forward(group).wait_recv()
    copies[2].wait()
    copies[3].wait()
    for at in range(2):
        suffix(at)
    other, top = turn(odd, top, chips + half, even)
    give_half(0, other)

    def first_messages():
        partials(0).wait_recv()
        send_groups(list(range(x_chips // 2)), tuple(own[which] for which in range(3)))

    other, top = turn(even, top, half, odd, first_messages)
    give_half(1, other)
    for at, piece in enumerate(pieces):
        own_second, _ = turn(odd, top[piece], None, None, piece=piece)
        if at == 0:
            partials(1).wait_recv()
        send_groups([x_chips // 2 + at], own_second)

    def whole(ref, count, send_sem, recv_sem):
        part = ref.at[pl.ds(0, count)]
        return pltpu.make_async_remote_copy(
            src_ref=part, dst_ref=part, send_sem=send_sem, recv_sem=recv_sem, device_id=(sibling, z), device_id_type=MESH
        )

    def arrived(part):
        count = half - 1 if part == 0 else half
        whole(got, count, msend, mrecv.at[part]).wait_recv()
        whole(gotstat, count, ssend, srecv.at[part]).wait_recv()
        blocks = slice(part * half, (part + 1) * half)
        sums = got[blocks].astype(F32)
        stats = jnp.broadcast_to(gotstat[blocks], sums.shape)
        tops, totals = (
            jnp.sum(jnp.where(diagonal(sums.shape, begin), stats, 0.0), axis=2, keepdims=True) for begin in (0, ROWS)
        )
        top = jnp.max(tops, axis=0, keepdims=True)
        factor = jnp.exp2(tops - top)
        return jnp.sum(sums * factor, axis=0), jnp.sum(totals * factor, axis=0), top[0]

    total_sum, total, _ = merged(arrived(0), arrived(1))
    result = total_sum / total
    wide = [jnp.concatenate([result[at * PER_GROUP + h][None] for h in range(PER_GROUP)], axis=1) for at in range(2)]
    zbuf[z] = jnp.concatenate(wide, axis=0).astype(BF16)

    def send_result(to):
        pltpu.make_async_remote_copy(
            src_ref=zbuf.at[z], dst_ref=zbuf.at[z], send_sem=zsend, recv_sem=zrecv, device_id=(seq, to), device_id_type=MESH
        ).start()

    others(z_chips, z, send_result)

    whole(qbuf, chips - 1, qsend, zrecv).wait_send()
    for group in range(x_chips):
        forward(group).wait_send()
    for part in range(2):
        partials(part).wait_send()
    whole(msg, chips - 1, msend, zrecv).wait_send()
    whole(stat, chips - 1, ssend, zrecv).wait_send()
    heads = whole(zbuf, z_chips - 1, zsend, zrecv)
    heads.wait_recv()
    out_ref[...] = zbuf[...]
    heads.wait_send()


def on_device(x_chips, *arrays):
    _, prefix_keys, _, suffix_keys, _, _, _ = arrays
    z_chips = lax.axis_size("head")
    chips = lax.axis_size("seq") // 2
    y_chips = chips // x_chips
    keys, cap = prefix_keys.shape[0], suffix_keys.shape[1]
    unit_rows = chips // 2 * ROWS
    chunk = min(1024, keys)
    hbm = pl.BlockSpec(memory_space=pltpu.MemorySpace.HBM)
    vmem = pl.BlockSpec(memory_space=pltpu.VMEM)
    smem = pl.BlockSpec(memory_space=pltpu.SMEM)
    dma = pltpu.SemaphoreType.DMA
    heads = pl.pallas_call(
        functools.partial(attend, x_chips, y_chips, z_chips, chunk),
        out_shape=pltpu.VMEM((z_chips, 2, PER_GROUP * HD), BF16),
        in_specs=[hbm, hbm, hbm, hbm, hbm, smem, smem],
        out_specs=vmem,
        scratch_shapes=[
            pltpu.VMEM((2, PER_GROUP * HD), BF16),
            pltpu.VMEM((ROWS, HD), BF16),
            pltpu.VMEM((2 * chips, ROWS, HD), BF16),
            pltpu.VMEM((keys, HD), BF16),
            pltpu.VMEM((keys, HD), BF16),
            pltpu.VMEM((2, cap, HD), BF16),
            pltpu.VMEM((2, cap, HD), BF16),
            pltpu.VMEM((unit_rows, keys), F32),
            pltpu.VMEM((unit_rows, keys), F32),
            pltpu.VMEM((3, unit_rows, HD), F32),
            pltpu.VMEM((2, 2, unit_rows, HD), F32),
            pltpu.VMEM((2, 2, unit_rows, HD), F32),
            pltpu.VMEM((2, 3, ROWS, HD), F32),
            pltpu.VMEM((chips, ROWS, HD), BF16),
            pltpu.VMEM((chips, ROWS, HD), BF16),
            pltpu.VMEM((chips, 1, HD), F32),
            pltpu.VMEM((chips, 1, HD), F32),
            pltpu.VMEM((z_chips, 2, PER_GROUP * HD), BF16),
            dma((5,)),
            dma,
            dma((x_chips,)),
            dma((x_chips,)),
            dma((x_chips,)),
            dma((2,)),
            dma((2,)),
            dma,
            dma((2,)),
            dma,
            dma((2,)),
            dma,
            dma,
        ],
        compiler_params=pltpu.CompilerParams(collective_id=0, has_side_effects=True, vmem_limit_bytes=56 << 20),
        name="attend",
    )(
        *(pltpu.with_memory_space_constraint(each, pltpu.MemorySpace.HBM) for each in arrays)
    )
    return jnp.swapaxes(heads, 0, 1).reshape(2, z_chips * PER_GROUP * HD)


def solution(mesh):
    in_specs = (
        P("seq", "head"),
        P("seq", "head"),
        P("seq", "head"),
        P("seq", None, "head"),
        P("seq", None, "head"),
        P("seq"),
        P("seq"),
    )
    return jax.shard_map(
        functools.partial(on_device, 4), mesh=mesh, in_specs=in_specs, out_specs=P("seq", None), check_vma=False
    )
```

```python
import functools
import math

import jax
import jax.numpy as jnp
from jax import lax
from jax.experimental import pallas as pl
from jax.experimental.pallas import tpu as pltpu
from jax.sharding import PartitionSpec as P

HD = 128
PER_GROUP = 8
NEG_BIG = -1e30
EXP2_SCALE = math.log2(math.e) / math.sqrt(HD)
ROWS = 16
F32 = jnp.float32
BF16 = jnp.bfloat16
MESH = pl.DeviceIdType.MESH


def attend(x_chips, y_chips, z_chips, chunk, q_ref, pk, pv, sk, sv, slen, sans, out_ref, qraw, qown, qbuf, keys_here, vbuf, skb, svb,
           even, odd, own, give, take, slot, msg, got, stat, gotstat, zbuf, local_sem, qsend, qrecv, fsend, frecv, psend, precv, msend, mrecv,
           ssend, srecv, zsend, zrecv):
    seq, z = lax.axis_index("seq"), lax.axis_index("head")
    chip = seq // 2
    core = seq - chip * 2
    x = chip // y_chips
    y = chip - x * y_chips
    sibling = chip * 2 + 1 - core
    chips = x_chips * y_chips
    half = chips // 2
    unit_rows = half * ROWS
    keys = keys_here.shape[0]

    def others(count, me, act):
        for step in range(1, count):
            act(lax.rem(me + step, count))

    copies = [
        pltpu.make_async_copy(pk, keys_here, local_sem.at[0]),
        pltpu.make_async_copy(pv, vbuf, local_sem.at[1]),
        pltpu.make_async_copy(sk, skb, local_sem.at[2]),
        pltpu.make_async_copy(sv, svb, local_sem.at[3]),
    ]
    query_copy = pltpu.make_async_copy(q_ref, qraw, local_sem.at[4])
    query_copy.start()

    barrier = pltpu.get_barrier_semaphore()

    def greet(to):
        pl.semaphore_signal(barrier, inc=1, device_id=to, device_id_type=MESH)

    columns = [lax.rem(x + group, x_chips) * y_chips for group in range(x_chips)]
    others(z_chips, z, lambda at: greet((seq, at)))
    for group in range(1, x_chips):
        for yy in range(y_chips):
            greet(((columns[group] + yy) * 2 + core, z))
    others(y_chips, y, lambda at: greet(((columns[0] + at) * 2 + core, z)))
    greet((sibling, z))
    for copy in copies:
        copy.start()

    query_copy.wait()
    raw = qraw[...].astype(F32)
    pieces = [raw[at : at + 1, h * HD : (h + 1) * HD] for at in range(2) for h in range(PER_GROUP)]
    block = jnp.concatenate(pieces, axis=0).astype(BF16)
    qown[...] = block
    qbuf[y] = block
    pl.semaphore_wait(barrier, 1 + (chips - 1) + (z_chips - 1))

    for group in range(x_chips):
        column = columns[(x_chips - group) % x_chips]

        def send_queries(yy, group=group, column=column):
            pltpu.make_async_remote_copy(
                src_ref=qown,
                dst_ref=qbuf.at[group * y_chips + y],
                send_sem=qsend,
                recv_sem=qrecv.at[group],
                device_id=((column + yy) * 2 + core, z),
                device_id_type=MESH,
            ).start()

        if group == 0:
            others(y_chips, y, send_queries)
        else:
            for yy in range(y_chips):
                send_queries(yy)

    copies[0].wait()

    def await_queries(group):
        first = 1 if group == 0 else 0
        part = qbuf.at[pl.ds(group * y_chips, y_chips - first)]
        pltpu.make_async_remote_copy(
            src_ref=part, dst_ref=part, send_sem=qsend, recv_sem=qrecv.at[group], device_id=(sibling, z), device_id_type=MESH
        ).wait_recv()

    def forward(group):
        return pltpu.make_async_remote_copy(
            src_ref=qbuf.at[pl.ds(group * y_chips, y_chips)],
            dst_ref=qbuf.at[pl.ds(chips + group * y_chips, y_chips)],
            send_sem=fsend.at[group],
            recv_sem=frecv.at[group],
            device_id=(sibling, z),
            device_id_type=MESH,
        )

    def partials(part):
        return pltpu.make_async_remote_copy(
            src_ref=give.at[part],
            dst_ref=take.at[part],
            send_sem=psend.at[part],
            recv_sem=precv.at[part],
            device_id=(sibling, z),
            device_id_type=MESH,
        )

    def stabiliser(scores_top):
        top = jnp.max(scores_top, axis=1, keepdims=True) * EXP2_SCALE
        return top.astype(BF16).astype(F32)

    def lane_tiles_max(scores):
        tiles = [scores[:, at : at + 128] for at in range(0, scores.shape[1], 128)]
        return functools.reduce(jnp.maximum, tiles)

    def weighted(scores, top, values):
        weights = jnp.exp2(scores * EXP2_SCALE - top).astype(BF16)
        wide = jnp.concatenate([values, jnp.ones(values.shape, BF16)], axis=1)
        return jnp.dot(weights, wide, preferred_element_type=F32)

    def inner(rows, columns):
        return lax.dot_general(rows, columns, (((1,), (1,)), ((), ())), preferred_element_type=F32)

    def turn(now, top, begin, later, midway=None, piece=None):
        span = slice(0, unit_rows) if piece is None else piece
        size = span.stop - span.start
        rows = None if begin is None else qbuf[begin : begin + size // ROWS].reshape(size, HD)

        def step(index, carry):
            both, later_top = carry
            at = pl.ds(pl.multiple_of(index * chunk, chunk), chunk)
            if begin is not None:
                scores = inner(rows, keys_here[at, :])
                later[span, at] = scores
                later_top = jnp.maximum(later_top, lane_tiles_max(scores))
            if now is not None:
                both = both + weighted(now[span, at], top, vbuf[at, :])
            return both, later_top

        count = keys // chunk
        carry = (
            None if now is None else jnp.zeros((size, 2 * HD), F32),
            None if begin is None else jnp.full((size, HD), 10 * NEG_BIG, F32),
        )
        if midway is None:
            both, later_top = lax.fori_loop(0, count, step, carry)
        else:
            carry = lax.fori_loop(0, count // 2, step, carry)
            midway()
            both, later_top = lax.fori_loop(count // 2, count, step, carry)
        part = None if now is None else (both[:, :HD], both[:, HD:], jnp.broadcast_to(top, (size, HD)))
        return part, None if begin is None else stabiliser(later_top)

    def suffix(at):
        holder = sans[at] // 2
        block = (holder + core) % 2 * chips + (holder // 2 - x * y_chips + chips) % chips
        scores = inner(qbuf[block], skb[at])
        position = lax.broadcasted_iota(jnp.int32, scores.shape, 1)
        scores = jnp.where(position < slen[at], scores, NEG_BIG)
        top = stabiliser(lane_tiles_max(scores))
        both = weighted(scores, top, svb[at])
        slot[at, 0] = both[:, :HD]
        slot[at, 1] = both[:, HD:]
        slot[at, 2] = jnp.broadcast_to(top, (ROWS, HD))

    def merged(first, second):
        top = jnp.maximum(first[2], second[2])
        one, two = jnp.exp2(first[2] - top), jnp.exp2(second[2] - top)
        return first[0] * one + second[0] * two, first[1] * one + second[1] * two, top

    def with_slots(value, first, mine):
        size = value[0].shape[0]
        shape = (size // ROWS, ROWS, HD)
        place = lax.broadcasted_iota(jnp.int32, shape, 0)
        second_row = jnp.where(lax.broadcasted_iota(jnp.int32, shape, 1) < PER_GROUP, 0, 1)
        at = place + (x * y_chips + first)
        at = jnp.where(at < chips, at, at - chips)
        answer = at * 4 + second_row + 2 * (core if mine else 1 - core)
        value = tuple(each.reshape(shape) for each in value)
        hits = [answer == sans[at] for at in range(2)]
        held = [[jnp.broadcast_to(slot[at, which][None], shape) for which in range(3)] for at in range(2)]
        piece = [jnp.where(hits[0], held[0][which], held[1][which]) for which in range(3)]
        piece[2] = jnp.where(hits[0], held[0][2], jnp.where(hits[1], held[1][2], NEG_BIG))
        return tuple(each.reshape(size, HD) for each in merged(value, piece))

    def give_half(part, value):
        total_sum, total, top = with_slots(value, part * half, False)
        lane = lax.broadcasted_iota(jnp.int32, total.shape, 1)
        give[part, 0] = total_sum
        give[part, 1] = jnp.where(lane < 64, top, total)
        partials(part).start()

    def diagonal(shape, begin):
        return lax.broadcasted_iota(jnp.int32, shape, 2) == lax.broadcasted_iota(jnp.int32, shape, 1) + begin

    def send_groups(groups, mine):
        first, size = groups[0] * y_chips, len(groups) * y_chips * ROWS
        part = first // half
        mine = with_slots(mine, first, True)
        span = slice((first - part * half) * ROWS, (first - part * half) * ROWS + size)
        stats = take[part, 1, span]
        theirs = (
            take[part, 0, span],
            jnp.broadcast_to(stats[:, 64:65], (size, HD)),
            jnp.broadcast_to(stats[:, 0:1], (size, HD)),
        )
        shape = (size // ROWS, ROWS, HD)
        total_sum, total, top = (each.reshape(shape) for each in merged(mine, theirs))
        blocks = slice(first, first + size // ROWS)
        msg[blocks] = total_sum.astype(BF16)
        row = jnp.where(diagonal(shape, 0), top, jnp.where(diagonal(shape, ROWS), total, 0.0))
        stat[blocks] = jnp.sum(row, axis=1, keepdims=True)
        for group in groups:

            def send(yy, group=group):
                to = ((columns[group] + yy) * 2 + core, z)
                for source, target, send_sem, recv_sem in ((msg, got, msend, mrecv), (stat, gotstat, ssend, srecv)):
                    pltpu.make_async_remote_copy(
                        src_ref=source.at[group * y_chips + yy],
                        dst_ref=target.at[group * y_chips + y],
                        send_sem=send_sem,
                        recv_sem=recv_sem.at[part],
                        device_id=to,
                        device_id_type=MESH,
                    ).start()

            if group == 0:
                others(y_chips, y, send)
                got[y] = msg[y]
                gotstat[y] = stat[y]
            else:
                for yy in range(y_chips):
                    send(yy)

    group_rows = y_chips * ROWS
    pieces = [slice(at, at + group_rows) for at in range(0, unit_rows, group_rows)]
    tops = []
    for group, piece in enumerate(pieces):
        await_queries(group)
        forward(group).start()
        tops.append(turn(None, None, group * y_chips, even, piece=piece)[1])
    top = jnp.concatenate(tops, axis=0)
    for group in range(x_chips // 2, x_chips):
        await_queries(group)
        forward(group).start()
    copies[1].wait()
    for group in range(x_chips // 2):
        forward(group).wait_recv()
    own_first, top = turn(even, top, chips, odd)
    for which in range(3):
        own[which] = own_first[which]
    for group in range(x_chips // 2, x_chips):
        forward(group).wait_recv()
    copies[2].wait()
    copies[3].wait()
    for at in range(2):
        suffix(at)
    other, top = turn(odd, top, chips + half, even)
    give_half(0, other)

    def first_messages():
        partials(0).wait_recv()
        send_groups(list(range(x_chips // 2)), tuple(own[which] for which in range(3)))

    other, top = turn(even, top, half, odd, first_messages)
    give_half(1, other)
    for at, piece in enumerate(pieces):
        own_second, _ = turn(odd, top[piece], None, None, piece=piece)
        if at == 0:
            partials(1).wait_recv()
        send_groups([x_chips // 2 + at], own_second)

    def whole(ref, count, send_sem, recv_sem):
        part = ref.at[pl.ds(0, count)]
        return pltpu.make_async_remote_copy(
            src_ref=part, dst_ref=part, send_sem=send_sem, recv_sem=recv_sem, device_id=(sibling, z), device_id_type=MESH
        )

    def arrived(part):
        count = half - 1 if part == 0 else half
        whole(got, count, msend, mrecv.at[part]).wait_recv()
        whole(gotstat, count, ssend, srecv.at[part]).wait_recv()
        blocks = slice(part * half, (part + 1) * half)
        sums = got[blocks].astype(F32)
        stats = jnp.broadcast_to(gotstat[blocks], sums.shape)
        tops, totals = (
            jnp.sum(jnp.where(diagonal(sums.shape, begin), stats, 0.0), axis=2, keepdims=True) for begin in (0, ROWS)
        )
        top = jnp.max(tops, axis=0, keepdims=True)
        factor = jnp.exp2(tops - top)
        return jnp.sum(sums * factor, axis=0), jnp.sum(totals * factor, axis=0), top[0]

    total_sum, total, _ = merged(arrived(0), arrived(1))
    result = total_sum / total
    wide = [jnp.concatenate([result[at * PER_GROUP + h][None] for h in range(PER_GROUP)], axis=1) for at in range(2)]
    zbuf[z] = jnp.concatenate(wide, axis=0).astype(BF16)

    def send_result(to):
        pltpu.make_async_remote_copy(
            src_ref=zbuf.at[z], dst_ref=zbuf.at[z], send_sem=zsend, recv_sem=zrecv, device_id=(seq, to), device_id_type=MESH
        ).start()

    others(z_chips, z, send_result)

    whole(qbuf, chips - 1, qsend, zrecv).wait_send()
    for group in range(x_chips):
        forward(group).wait_send()
    for part in range(2):
        partials(part).wait_send()
    whole(msg, chips - 1, msend, zrecv).wait_send()
    whole(stat, chips - 1, ssend, zrecv).wait_send()
    heads = whole(zbuf, z_chips - 1, zsend, zrecv)
    heads.wait_recv()
    out_ref[...] = zbuf[...]
    heads.wait_send()


def on_device(x_chips, *arrays):
    _, prefix_keys, _, suffix_keys, _, _, _ = arrays
    z_chips = lax.axis_size("head")
    chips = lax.axis_size("seq") // 2
    y_chips = chips // x_chips
    keys, cap = prefix_keys.shape[0], suffix_keys.shape[1]
    unit_rows = chips // 2 * ROWS
    chunk = min(1024, keys)
    hbm = pl.BlockSpec(memory_space=pltpu.MemorySpace.HBM)
    vmem = pl.BlockSpec(memory_space=pltpu.VMEM)
    smem = pl.BlockSpec(memory_space=pltpu.SMEM)
    dma = pltpu.SemaphoreType.DMA
    heads = pl.pallas_call(
        functools.partial(attend, x_chips, y_chips, z_chips, chunk),
        out_shape=pltpu.VMEM((z_chips, 2, PER_GROUP * HD), BF16),
        in_specs=[hbm, hbm, hbm, hbm, hbm, smem, smem],
        out_specs=vmem,
        scratch_shapes=[
            pltpu.VMEM((2, PER_GROUP * HD), BF16),
            pltpu.VMEM((ROWS, HD), BF16),
            pltpu.VMEM((2 * chips, ROWS, HD), BF16),
            pltpu.VMEM((keys, HD), BF16),
            pltpu.VMEM((keys, HD), BF16),
            pltpu.VMEM((2, cap, HD), BF16),
            pltpu.VMEM((2, cap, HD), BF16),
            pltpu.VMEM((unit_rows, keys), F32),
            pltpu.VMEM((unit_rows, keys), F32),
            pltpu.VMEM((3, unit_rows, HD), F32),
            pltpu.VMEM((2, 2, unit_rows, HD), F32),
            pltpu.VMEM((2, 2, unit_rows, HD), F32),
            pltpu.VMEM((2, 3, ROWS, HD), F32),
            pltpu.VMEM((chips, ROWS, HD), BF16),
            pltpu.VMEM((chips, ROWS, HD), BF16),
            pltpu.VMEM((chips, 1, HD), F32),
            pltpu.VMEM((chips, 1, HD), F32),
            pltpu.VMEM((z_chips, 2, PER_GROUP * HD), BF16),
            dma((5,)),
            dma,
            dma((x_chips,)),
            dma((x_chips,)),
            dma((x_chips,)),
            dma((2,)),
            dma((2,)),
            dma,
            dma((2,)),
            dma,
            dma((2,)),
            dma,
            dma,
        ],
        compiler_params=pltpu.CompilerParams(collective_id=0, has_side_effects=True, vmem_limit_bytes=56 << 20),
        name="attend",
    )(
        *(pltpu.with_memory_space_constraint(each, pltpu.MemorySpace.HBM) for each in arrays)
    )
    return jnp.swapaxes(heads, 0, 1).reshape(2, z_chips * PER_GROUP * HD)


def solution(mesh):
    in_specs = (
        P("seq", "head"),
        P("seq", "head"),
        P("seq", "head"),
        P("seq", None, "head"),
        P("seq", None, "head"),
        P("seq"),
        P("seq"),
    )
    return jax.shard_map(
        functools.partial(on_device, 4), mesh=mesh, in_specs=in_specs, out_specs=P("seq", None), check_vma=False
    )
```

```python
import functools
import math

import jax
import jax.numpy as jnp
from jax import lax
from jax.experimental import pallas as pl
from jax.experimental.pallas import tpu as pltpu
from jax.sharding import PartitionSpec as P

HD = 128
PER_GROUP = 8
NEG_BIG = -1e30
EXP2_SCALE = math.log2(math.e) / math.sqrt(HD)
ROWS = 16
F32 = jnp.float32
BF16 = jnp.bfloat16
MESH = pl.DeviceIdType.MESH


def attend(x_chips, y_chips, z_chips, chunk, q_ref, pk, pv, sk, sv, slen, sans, out_ref, qraw, qown, qbuf, keys_here, vbuf, skb, svb,
           even, odd, own, give, take, slot, msg, got, stat, gotstat, zbuf, local_sem, qsend, qrecv, fsend, frecv, psend, precv, msend, mrecv,
           ssend, srecv, zsend, zrecv):
    seq, z = lax.axis_index("seq"), lax.axis_index("head")
    chip = seq // 2
    core = seq - chip * 2
    x = chip // y_chips
    y = chip - x * y_chips
    sibling = chip * 2 + 1 - core
    chips = x_chips * y_chips
    half = chips // 2
    unit_rows = half * ROWS
    keys = keys_here.shape[0]

    def others(count, me, act):
        for step in range(1, count):
            act(lax.rem(me + step, count))

    copies = [
        pltpu.make_async_copy(pk, keys_here, local_sem.at[0]),
        pltpu.make_async_copy(pv, vbuf, local_sem.at[1]),
        pltpu.make_async_copy(sk, skb, local_sem.at[2]),
        pltpu.make_async_copy(sv, svb, local_sem.at[3]),
    ]
    query_copy = pltpu.make_async_copy(q_ref, qraw, local_sem.at[4])
    query_copy.start()

    barrier = pltpu.get_barrier_semaphore()

    def greet(to):
        pl.semaphore_signal(barrier, inc=1, device_id=to, device_id_type=MESH)

    columns = [lax.rem(x + group, x_chips) * y_chips for group in range(x_chips)]
    others(z_chips, z, lambda at: greet((seq, at)))
    for group in range(1, x_chips):
        for yy in range(y_chips):
            greet(((columns[group] + yy) * 2 + core, z))
    others(y_chips, y, lambda at: greet(((columns[0] + at) * 2 + core, z)))
    greet((sibling, z))
    for copy in copies:
        copy.start()

    query_copy.wait()
    raw = qraw[...].astype(F32)
    pieces = [raw[at : at + 1, h * HD : (h + 1) * HD] for at in range(2) for h in range(PER_GROUP)]
    block = jnp.concatenate(pieces, axis=0).astype(BF16)
    qown[...] = block
    qbuf[y] = block
    pl.semaphore_wait(barrier, 1 + (chips - 1) + (z_chips - 1))

    for group in range(x_chips):
        column = columns[(x_chips - group) % x_chips]

        def send_queries(yy, group=group, column=column):
            pltpu.make_async_remote_copy(
                src_ref=qown,
                dst_ref=qbuf.at[group * y_chips + y],
                send_sem=qsend,
                recv_sem=qrecv.at[group],
                device_id=((column + yy) * 2 + core, z),
                device_id_type=MESH,
            ).start()

        if group == 0:
            others(y_chips, y, send_queries)
        else:
            for yy in range(y_chips):
                send_queries(yy)

    copies[0].wait()

    def await_queries(group):
        first = 1 if group == 0 else 0
        part = qbuf.at[pl.ds(group * y_chips, y_chips - first)]
        pltpu.make_async_remote_copy(
            src_ref=part, dst_ref=part, send_sem=qsend, recv_sem=qrecv.at[group], device_id=(sibling, z), device_id_type=MESH
        ).wait_recv()

    def forward(group):
        return pltpu.make_async_remote_copy(
            src_ref=qbuf.at[pl.ds(group * y_chips, y_chips)],
            dst_ref=qbuf.at[pl.ds(chips + group * y_chips, y_chips)],
            send_sem=fsend.at[group],
            recv_sem=frecv.at[group],
            device_id=(sibling, z),
            device_id_type=MESH,
        )

    def partials(part):
        return pltpu.make_async_remote_copy(
            src_ref=give.at[part],
            dst_ref=take.at[part],
            send_sem=psend.at[part],
            recv_sem=precv.at[part],
            device_id=(sibling, z),
            device_id_type=MESH,
        )

    def stabiliser(scores_top):
        top = jnp.max(scores_top, axis=1, keepdims=True) * EXP2_SCALE
        return top.astype(BF16).astype(F32)

    def lane_tiles_max(scores):
        tiles = [scores[:, at : at + 128] for at in range(0, scores.shape[1], 128)]
        return functools.reduce(jnp.maximum, tiles)

    def weighted(scores, top, values):
        weights = jnp.exp2(scores * EXP2_SCALE - top).astype(BF16)
        wide = jnp.concatenate([values, jnp.ones(values.shape, BF16)], axis=1)
        return jnp.dot(weights, wide, preferred_element_type=F32)

    def inner(rows, columns):
        return lax.dot_general(rows, columns, (((1,), (1,)), ((), ())), preferred_element_type=F32)

    def turn(now, top, begin, later, midway=None, piece=None):
        both, later_top = None, None
        span = slice(0, unit_rows) if piece is None else piece
        size = span.stop - span.start
        rows = None if begin is None else qbuf[begin : begin + size // ROWS].reshape(size, HD)
        for at in range(0, keys, chunk):
            if midway is not None and at == keys // 2:
                midway()
            if begin is not None:
                scores = inner(rows, keys_here[at : at + chunk, :])
                later[span, at : at + chunk] = scores
                here = lane_tiles_max(scores)
                later_top = here if later_top is None else jnp.maximum(later_top, here)
            if now is not None:
                here = weighted(now[span, at : at + chunk], top, vbuf[at : at + chunk, :])
                both = here if both is None else both + here
        part = None if now is None else (both[:, :HD], both[:, HD:], jnp.broadcast_to(top, (size, HD)))
        return part, None if begin is None else stabiliser(later_top)

    def suffix(at):
        holder = sans[at] // 2
        block = (holder + core) % 2 * chips + (holder // 2 - x * y_chips + chips) % chips
        scores = inner(qbuf[block], skb[at])
        position = lax.broadcasted_iota(jnp.int32, scores.shape, 1)
        scores = jnp.where(position < slen[at], scores, NEG_BIG)
        top = stabiliser(lane_tiles_max(scores))
        both = weighted(scores, top, svb[at])
        slot[at, 0] = both[:, :HD]
        slot[at, 1] = both[:, HD:]
        slot[at, 2] = jnp.broadcast_to(top, (ROWS, HD))

    def merged(first, second):
        top = jnp.maximum(first[2], second[2])
        one, two = jnp.exp2(first[2] - top), jnp.exp2(second[2] - top)
        return first[0] * one + second[0] * two, first[1] * one + second[1] * two, top

    def with_slots(value, first, mine):
        size = value[0].shape[0]
        shape = (size // ROWS, ROWS, HD)
        place = lax.broadcasted_iota(jnp.int32, shape, 0)
        second_row = jnp.where(lax.broadcasted_iota(jnp.int32, shape, 1) < PER_GROUP, 0, 1)
        at = place + (x * y_chips + first)
        at = jnp.where(at < chips, at, at - chips)
        answer = at * 4 + second_row + 2 * (core if mine else 1 - core)
        value = tuple(each.reshape(shape) for each in value)
        hits = [answer == sans[at] for at in range(2)]
        held = [[jnp.broadcast_to(slot[at, which][None], shape) for which in range(3)] for at in range(2)]
        piece = [jnp.where(hits[0], held[0][which], held[1][which]) for which in range(3)]
        piece[2] = jnp.where(hits[0], held[0][2], jnp.where(hits[1], held[1][2], NEG_BIG))
        return tuple(each.reshape(size, HD) for each in merged(value, piece))

    def give_half(part, value):
        total_sum, total, top = with_slots(value, part * half, False)
        lane = lax.broadcasted_iota(jnp.int32, total.shape, 1)
        give[part, 0] = total_sum
        give[part, 1] = jnp.where(lane < 64, top, total)
        partials(part).start()

    def diagonal(shape, begin):
        return lax.broadcasted_iota(jnp.int32, shape, 2) == lax.broadcasted_iota(jnp.int32, shape, 1) + begin

    def send_groups(groups, mine):
        first, size = groups[0] * y_chips, len(groups) * y_chips * ROWS
        part = first // half
        mine = with_slots(mine, first, True)
        span = slice((first - part * half) * ROWS, (first - part * half) * ROWS + size)
        stats = take[part, 1, span]
        theirs = (
            take[part, 0, span],
            jnp.broadcast_to(stats[:, 64:65], (size, HD)),
            jnp.broadcast_to(stats[:, 0:1], (size, HD)),
        )
        shape = (size // ROWS, ROWS, HD)
        total_sum, total, top = (each.reshape(shape) for each in merged(mine, theirs))
        blocks = slice(first, first + size // ROWS)
        msg[blocks] = total_sum.astype(BF16)
        row = jnp.where(diagonal(shape, 0), top, jnp.where(diagonal(shape, ROWS), total, 0.0))
        stat[blocks] = jnp.sum(row, axis=1, keepdims=True)
        for group in groups:

            def send(yy, group=group):
                to = ((columns[group] + yy) * 2 + core, z)
                for source, target, send_sem, recv_sem in ((msg, got, msend, mrecv), (stat, gotstat, ssend, srecv)):
                    pltpu.make_async_remote_copy(
                        src_ref=source.at[group * y_chips + yy],
                        dst_ref=target.at[group * y_chips + y],
                        send_sem=send_sem,
                        recv_sem=recv_sem.at[part],
                        device_id=to,
                        device_id_type=MESH,
                    ).start()

            if group == 0:
                others(y_chips, y, send)
                got[y] = msg[y]
                gotstat[y] = stat[y]
            else:
                for yy in range(y_chips):
                    send(yy)

    group_rows = y_chips * ROWS
    pieces = [slice(at, at + group_rows) for at in range(0, unit_rows, group_rows)]
    tops = []
    for group, piece in enumerate(pieces):
        await_queries(group)
        forward(group).start()
        tops.append(turn(None, None, group * y_chips, even, piece=piece)[1])
    top = jnp.concatenate(tops, axis=0)
    for group in range(x_chips // 2, x_chips):
        await_queries(group)
        forward(group).start()
    copies[1].wait()
    for group in range(x_chips // 2):
        forward(group).wait_recv()
    own_first, top = turn(even, top, chips, odd)
    for which in range(3):
        own[which] = own_first[which]
    for group in range(x_chips // 2, x_chips):
        forward(group).wait_recv()
    copies[2].wait()
    copies[3].wait()
    for at in range(2):
        suffix(at)
    other, top = turn(odd, top, chips + half, even)
    give_half(0, other)

    def first_messages():
        partials(0).wait_recv()
        send_groups(list(range(x_chips // 2)), tuple(own[which] for which in range(3)))

    other, top = turn(even, top, half, odd, first_messages)
    give_half(1, other)
    for at, piece in enumerate(pieces):
        own_second, _ = turn(odd, top[piece], None, None, piece=piece)
        if at == 0:
            partials(1).wait_recv()
        send_groups([x_chips // 2 + at], own_second)

    def whole(ref, count, send_sem, recv_sem):
        part = ref.at[pl.ds(0, count)]
        return pltpu.make_async_remote_copy(
            src_ref=part, dst_ref=part, send_sem=send_sem, recv_sem=recv_sem, device_id=(sibling, z), device_id_type=MESH
        )

    def arrived(part):
        count = half - 1 if part == 0 else half
        whole(got, count, msend, mrecv.at[part]).wait_recv()
        whole(gotstat, count, ssend, srecv.at[part]).wait_recv()
        blocks = slice(part * half, (part + 1) * half)
        sums = got[blocks].astype(F32)
        stats = jnp.broadcast_to(gotstat[blocks], sums.shape)
        tops, totals = (
            jnp.sum(jnp.where(diagonal(sums.shape, begin), stats, 0.0), axis=2, keepdims=True) for begin in (0, ROWS)
        )
        top = jnp.max(tops, axis=0, keepdims=True)
        factor = jnp.exp2(tops - top)
        return jnp.sum(sums * factor, axis=0), jnp.sum(totals * factor, axis=0), top[0]

    total_sum, total, _ = merged(arrived(0), arrived(1))
    result = total_sum / total
    wide = [jnp.concatenate([result[at * PER_GROUP + h][None] for h in range(PER_GROUP)], axis=1) for at in range(2)]
    zbuf[z] = jnp.concatenate(wide, axis=0).astype(BF16)

    def send_result(to):
        pltpu.make_async_remote_copy(
            src_ref=zbuf.at[z], dst_ref=zbuf.at[z], send_sem=zsend, recv_sem=zrecv, device_id=(seq, to), device_id_type=MESH
        ).start()

    others(z_chips, z, send_result)

    whole(qbuf, chips - 1, qsend, zrecv).wait_send()
    for group in range(x_chips):
        forward(group).wait_send()
    for part in range(2):
        partials(part).wait_send()
    whole(msg, chips - 1, msend, zrecv).wait_send()
    whole(stat, chips - 1, ssend, zrecv).wait_send()
    heads = whole(zbuf, z_chips - 1, zsend, zrecv)
    heads.wait_recv()
    out_ref[...] = zbuf[...]
    heads.wait_send()


def on_device(x_chips, *arrays):
    _, prefix_keys, _, suffix_keys, _, _, _ = arrays
    z_chips = lax.axis_size("head")
    chips = lax.axis_size("seq") // 2
    y_chips = chips // x_chips
    keys, cap = prefix_keys.shape[0], suffix_keys.shape[1]
    unit_rows = chips // 2 * ROWS
    chunk = min(256, keys)
    hbm = pl.BlockSpec(memory_space=pltpu.MemorySpace.HBM)
    vmem = pl.BlockSpec(memory_space=pltpu.VMEM)
    smem = pl.BlockSpec(memory_space=pltpu.SMEM)
    dma = pltpu.SemaphoreType.DMA
    heads = pl.pallas_call(
        functools.partial(attend, x_chips, y_chips, z_chips, chunk),
        out_shape=pltpu.VMEM((z_chips, 2, PER_GROUP * HD), BF16),
        in_specs=[hbm, hbm, hbm, hbm, hbm, smem, smem],
        out_specs=vmem,
        scratch_shapes=[
            pltpu.VMEM((2, PER_GROUP * HD), BF16),
            pltpu.VMEM((ROWS, HD), BF16),
            pltpu.VMEM((2 * chips, ROWS, HD), BF16),
            pltpu.VMEM((keys, HD), BF16),
            pltpu.VMEM((keys, HD), BF16),
            pltpu.VMEM((2, cap, HD), BF16),
            pltpu.VMEM((2, cap, HD), BF16),
            pltpu.VMEM((unit_rows, keys), F32),
            pltpu.VMEM((unit_rows, keys), F32),
            pltpu.VMEM((3, unit_rows, HD), F32),
            pltpu.VMEM((2, 2, unit_rows, HD), F32),
            pltpu.VMEM((2, 2, unit_rows, HD), F32),
            pltpu.VMEM((2, 3, ROWS, HD), F32),
            pltpu.VMEM((chips, ROWS, HD), BF16),
            pltpu.VMEM((chips, ROWS, HD), BF16),
            pltpu.VMEM((chips, 1, HD), F32),
            pltpu.VMEM((chips, 1, HD), F32),
            pltpu.VMEM((z_chips, 2, PER_GROUP * HD), BF16),
            dma((5,)),
            dma,
            dma((x_chips,)),
            dma((x_chips,)),
            dma((x_chips,)),
            dma((2,)),
            dma((2,)),
            dma,
            dma((2,)),
            dma,
            dma((2,)),
            dma,
            dma,
        ],
        compiler_params=pltpu.CompilerParams(collective_id=0, has_side_effects=True, vmem_limit_bytes=56 << 20),
        name="attend",
    )(
        *(pltpu.with_memory_space_constraint(each, pltpu.MemorySpace.HBM) for each in arrays)
    )
    return jnp.swapaxes(heads, 0, 1).reshape(2, z_chips * PER_GROUP * HD)


def solution(mesh):
    in_specs = (
        P("seq", "head"),
        P("seq", "head"),
        P("seq", "head"),
        P("seq", None, "head"),
        P("seq", None, "head"),
        P("seq"),
        P("seq"),
    )
    return jax.shard_map(
        functools.partial(on_device, 4), mesh=mesh, in_specs=in_specs, out_specs=P("seq", None), check_vma=False
    )
```

```python
import functools
import math

import jax
import jax.numpy as jnp
from jax import lax
from jax.experimental import pallas as pl
from jax.experimental.pallas import tpu as pltpu
from jax.sharding import PartitionSpec as P

HD = 128
PER_GROUP = 8
NEG_BIG = -1e30
EXP2_SCALE = math.log2(math.e) / math.sqrt(HD)
ROWS = 16
F32 = jnp.float32
BF16 = jnp.bfloat16
MESH = pl.DeviceIdType.MESH


def attend(x_chips, y_chips, z_chips, chunk, q_ref, pk, pv, sk, sv, slen, sans, out_ref, qraw, qown, qbuf, keys_here, vbuf, skb, svb,
           even, odd, own, give, take, slot, msg, got, stat, gotstat, zbuf, local_sem, qsend, qrecv, fsend, frecv, psend, precv, msend, mrecv,
           ssend, srecv, zsend, zrecv):
    seq, z = lax.axis_index("seq"), lax.axis_index("head")
    chip = seq // 2
    core = seq - chip * 2
    x = chip // y_chips
    y = chip - x * y_chips
    sibling = chip * 2 + 1 - core
    chips = x_chips * y_chips
    half = chips // 2
    unit_rows = half * ROWS
    keys = keys_here.shape[0]

    def others(count, me, act):
        for step in range(1, count):
            act(lax.rem(me + step, count))

    copies = [
        pltpu.make_async_copy(pk, keys_here, local_sem.at[0]),
        pltpu.make_async_copy(pv, vbuf, local_sem.at[1]),
        pltpu.make_async_copy(sk, skb, local_sem.at[2]),
        pltpu.make_async_copy(sv, svb, local_sem.at[3]),
    ]
    query_copy = pltpu.make_async_copy(q_ref, qraw, local_sem.at[4])
    query_copy.start()

    barrier = pltpu.get_barrier_semaphore()

    def greet(to):
        pl.semaphore_signal(barrier, inc=1, device_id=to, device_id_type=MESH)

    columns = [lax.rem(x + group, x_chips) * y_chips for group in range(x_chips)]
    others(z_chips, z, lambda at: greet((seq, at)))
    for group in range(1, x_chips):
        for yy in range(y_chips):
            greet(((columns[group] + yy) * 2 + core, z))
    others(y_chips, y, lambda at: greet(((columns[0] + at) * 2 + core, z)))
    greet((sibling, z))
    for copy in copies:
        copy.start()

    query_copy.wait()
    raw = qraw[...].astype(F32)
    pieces = [raw[at : at + 1, h * HD : (h + 1) * HD] for at in range(2) for h in range(PER_GROUP)]
    block = jnp.concatenate(pieces, axis=0).astype(BF16)
    qown[...] = block
    qbuf[y] = block
    pl.semaphore_wait(barrier, 1 + (chips - 1) + (z_chips - 1))

    for group in range(x_chips):
        column = columns[(x_chips - group) % x_chips]

        def send_queries(yy, group=group, column=column):
            pltpu.make_async_remote_copy(
                src_ref=qown,
                dst_ref=qbuf.at[group * y_chips + y],
                send_sem=qsend,
                recv_sem=qrecv.at[group],
                device_id=((column + yy) * 2 + core, z),
                device_id_type=MESH,
            ).start()

        if group == 0:
            others(y_chips, y, send_queries)
        else:
            for yy in range(y_chips):
                send_queries(yy)

    copies[0].wait()

    def await_queries(group):
        first = 1 if group == 0 else 0
        part = qbuf.at[pl.ds(group * y_chips, y_chips - first)]
        pltpu.make_async_remote_copy(
            src_ref=part, dst_ref=part, send_sem=qsend, recv_sem=qrecv.at[group], device_id=(sibling, z), device_id_type=MESH
        ).wait_recv()

    def forward(group):
        return pltpu.make_async_remote_copy(
            src_ref=qbuf.at[pl.ds(group * y_chips, y_chips)],
            dst_ref=qbuf.at[pl.ds(chips + group * y_chips, y_chips)],
            send_sem=fsend.at[group],
            recv_sem=frecv.at[group],
            device_id=(sibling, z),
            device_id_type=MESH,
        )

    def partials(part):
        return pltpu.make_async_remote_copy(
            src_ref=give.at[part],
            dst_ref=take.at[part],
            send_sem=psend.at[part],
            recv_sem=precv.at[part],
            device_id=(sibling, z),
            device_id_type=MESH,
        )

    def stabiliser(scores_top):
        top = jnp.max(scores_top, axis=1, keepdims=True) * EXP2_SCALE
        return top.astype(BF16).astype(F32)

    def lane_tiles_max(scores):
        tiles = [scores[:, at : at + 128] for at in range(0, scores.shape[1], 128)]
        return functools.reduce(jnp.maximum, tiles)

    def weighted(scores, top, values):
        weights = jnp.exp2(scores * EXP2_SCALE - top).astype(BF16)
        wide = jnp.concatenate([values, jnp.ones(values.shape, BF16)], axis=1)
        return jnp.dot(weights, wide, preferred_element_type=F32)

    def inner(rows, columns):
        return lax.dot_general(rows, columns, (((1,), (1,)), ((), ())), preferred_element_type=F32)

    def turn(now, top, begin, later, midway=None, piece=None):
        both, later_top = None, None
        span = slice(0, unit_rows) if piece is None else piece
        size = span.stop - span.start
        rows = None if begin is None else qbuf[begin : begin + size // ROWS].reshape(size, HD)
        for at in range(0, keys, chunk):
            if midway is not None and at == keys // 2:
                midway()
            if begin is not None:
                scores = inner(rows, keys_here[at : at + chunk, :])
                later[span, at : at + chunk] = scores
                here = lane_tiles_max(scores)
                later_top = here if later_top is None else jnp.maximum(later_top, here)
            if now is not None:
                here = weighted(now[span, at : at + chunk], top, vbuf[at : at + chunk, :])
                both = here if both is None else both + here
        part = None if now is None else (both[:, :HD], both[:, HD:], jnp.broadcast_to(top, (size, HD)))
        return part, None if begin is None else stabiliser(later_top)

    def suffix(at):
        holder = sans[at] // 2
        block = (holder + core) % 2 * chips + (holder // 2 - x * y_chips + chips) % chips
        scores = inner(qbuf[block], skb[at])
        position = lax.broadcasted_iota(jnp.int32, scores.shape, 1)
        scores = jnp.where(position < slen[at], scores, NEG_BIG)
        top = stabiliser(lane_tiles_max(scores))
        both = weighted(scores, top, svb[at])
        slot[at, 0] = both[:, :HD]
        slot[at, 1] = both[:, HD:]
        slot[at, 2] = jnp.broadcast_to(top, (ROWS, HD))

    def merged(first, second):
        top = jnp.maximum(first[2], second[2])
        one, two = jnp.exp2(first[2] - top), jnp.exp2(second[2] - top)
        return first[0] * one + second[0] * two, first[1] * one + second[1] * two, top

    def with_slots(value, first, mine):
        size = value[0].shape[0]
        shape = (size // ROWS, ROWS, HD)
        place = lax.broadcasted_iota(jnp.int32, shape, 0)
        second_row = jnp.where(lax.broadcasted_iota(jnp.int32, shape, 1) < PER_GROUP, 0, 1)
        at = place + (x * y_chips + first)
        at = jnp.where(at < chips, at, at - chips)
        answer = at * 4 + second_row + 2 * (core if mine else 1 - core)
        value = tuple(each.reshape(shape) for each in value)
        hits = [answer == sans[at] for at in range(2)]
        held = [[jnp.broadcast_to(slot[at, which][None], shape) for which in range(3)] for at in range(2)]
        piece = [jnp.where(hits[0], held[0][which], held[1][which]) for which in range(3)]
        piece[2] = jnp.where(hits[0], held[0][2], jnp.where(hits[1], held[1][2], NEG_BIG))
        return tuple(each.reshape(size, HD) for each in merged(value, piece))

    def give_half(part, value):
        total_sum, total, top = with_slots(value, part * half, False)
        lane = lax.broadcasted_iota(jnp.int32, total.shape, 1)
        give[part, 0] = total_sum
        give[part, 1] = jnp.where(lane < 64, top, total)
        partials(part).start()

    def diagonal(shape, begin):
        return lax.broadcasted_iota(jnp.int32, shape, 2) == lax.broadcasted_iota(jnp.int32, shape, 1) + begin

    def send_groups(groups, mine):
        first, size = groups[0] * y_chips, len(groups) * y_chips * ROWS
        part = first // half
        mine = with_slots(mine, first, True)
        span = slice((first - part * half) * ROWS, (first - part * half) * ROWS + size)
        stats = take[part, 1, span]
        theirs = (
            take[part, 0, span],
            jnp.broadcast_to(stats[:, 64:65], (size, HD)),
            jnp.broadcast_to(stats[:, 0:1], (size, HD)),
        )
        shape = (size // ROWS, ROWS, HD)
        total_sum, total, top = (each.reshape(shape) for each in merged(mine, theirs))
        blocks = slice(first, first + size // ROWS)
        msg[blocks] = total_sum.astype(BF16)
        row = jnp.where(diagonal(shape, 0), top, jnp.where(diagonal(shape, ROWS), total, 0.0))
        stat[blocks] = jnp.sum(row, axis=1, keepdims=True)
        for group in groups:

            def send(yy, group=group):
                to = ((columns[group] + yy) * 2 + core, z)
                for source, target, send_sem, recv_sem in ((msg, got, msend, mrecv), (stat, gotstat, ssend, srecv)):
                    pltpu.make_async_remote_copy(
                        src_ref=source.at[group * y_chips + yy],
                        dst_ref=target.at[group * y_chips + y],
                        send_sem=send_sem,
                        recv_sem=recv_sem.at[part],
                        device_id=to,
                        device_id_type=MESH,
                    ).start()

            if group == 0:
                others(y_chips, y, send)
                got[y] = msg[y]
                gotstat[y] = stat[y]
            else:
                for yy in range(y_chips):
                    send(yy)

    group_rows = y_chips * ROWS
    pieces = [slice(at, at + group_rows) for at in range(0, unit_rows, group_rows)]
    tops = []
    for group, piece in enumerate(pieces):
        await_queries(group)
        forward(group).start()
        tops.append(turn(None, None, group * y_chips, even, piece=piece)[1])
    top = jnp.concatenate(tops, axis=0)
    for group in range(x_chips // 2, x_chips):
        await_queries(group)
        forward(group).start()
    copies[1].wait()
    for group in range(x_chips // 2):
        forward(group).wait_recv()
    own_first, top = turn(even, top, chips, odd)
    for which in range(3):
        own[which] = own_first[which]
    for group in range(x_chips // 2, x_chips):
        forward(group).wait_recv()
    copies[2].wait()
    copies[3].wait()
    other, top = turn(odd, top, chips + half, even, lambda: [suffix(at) for at in range(2)])
    give_half(0, other)

    def first_messages():
        partials(0).wait_recv()
        send_groups(list(range(x_chips // 2)), tuple(own[which] for which in range(3)))

    other, top = turn(even, top, half, odd, first_messages)
    give_half(1, other)
    for at, piece in enumerate(pieces):
        own_second, _ = turn(odd, top[piece], None, None, piece=piece)
        if at == 0:
            partials(1).wait_recv()
        send_groups([x_chips // 2 + at], own_second)

    def whole(ref, count, send_sem, recv_sem):
        part = ref.at[pl.ds(0, count)]
        return pltpu.make_async_remote_copy(
            src_ref=part, dst_ref=part, send_sem=send_sem, recv_sem=recv_sem, device_id=(sibling, z), device_id_type=MESH
        )

    def arrived(part):
        count = half - 1 if part == 0 else half
        whole(got, count, msend, mrecv.at[part]).wait_recv()
        whole(gotstat, count, ssend, srecv.at[part]).wait_recv()
        blocks = slice(part * half, (part + 1) * half)
        sums = got[blocks].astype(F32)
        stats = jnp.broadcast_to(gotstat[blocks], sums.shape)
        tops, totals = (
            jnp.sum(jnp.where(diagonal(sums.shape, begin), stats, 0.0), axis=2, keepdims=True) for begin in (0, ROWS)
        )
        top = jnp.max(tops, axis=0, keepdims=True)
        factor = jnp.exp2(tops - top)
        return jnp.sum(sums * factor, axis=0), jnp.sum(totals * factor, axis=0), top[0]

    total_sum, total, _ = merged(arrived(0), arrived(1))
    result = total_sum / total
    wide = [jnp.concatenate([result[at * PER_GROUP + h][None] for h in range(PER_GROUP)], axis=1) for at in range(2)]
    zbuf[z] = jnp.concatenate(wide, axis=0).astype(BF16)

    def send_result(to):
        pltpu.make_async_remote_copy(
            src_ref=zbuf.at[z], dst_ref=zbuf.at[z], send_sem=zsend, recv_sem=zrecv, device_id=(seq, to), device_id_type=MESH
        ).start()

    others(z_chips, z, send_result)

    whole(qbuf, chips - 1, qsend, zrecv).wait_send()
    for group in range(x_chips):
        forward(group).wait_send()
    for part in range(2):
        partials(part).wait_send()
    whole(msg, chips - 1, msend, zrecv).wait_send()
    whole(stat, chips - 1, ssend, zrecv).wait_send()
    heads = whole(zbuf, z_chips - 1, zsend, zrecv)
    heads.wait_recv()
    out_ref[...] = zbuf[...]
    heads.wait_send()


def on_device(x_chips, *arrays):
    _, prefix_keys, _, suffix_keys, _, _, _ = arrays
    z_chips = lax.axis_size("head")
    chips = lax.axis_size("seq") // 2
    y_chips = chips // x_chips
    keys, cap = prefix_keys.shape[0], suffix_keys.shape[1]
    unit_rows = chips // 2 * ROWS
    chunk = min(256, keys)
    hbm = pl.BlockSpec(memory_space=pltpu.MemorySpace.HBM)
    vmem = pl.BlockSpec(memory_space=pltpu.VMEM)
    smem = pl.BlockSpec(memory_space=pltpu.SMEM)
    dma = pltpu.SemaphoreType.DMA
    heads = pl.pallas_call(
        functools.partial(attend, x_chips, y_chips, z_chips, chunk),
        out_shape=pltpu.VMEM((z_chips, 2, PER_GROUP * HD), BF16),
        in_specs=[hbm, hbm, hbm, hbm, hbm, smem, smem],
        out_specs=vmem,
        scratch_shapes=[
            pltpu.VMEM((2, PER_GROUP * HD), BF16),
            pltpu.VMEM((ROWS, HD), BF16),
            pltpu.VMEM((2 * chips, ROWS, HD), BF16),
            pltpu.VMEM((keys, HD), BF16),
            pltpu.VMEM((keys, HD), BF16),
            pltpu.VMEM((2, cap, HD), BF16),
            pltpu.VMEM((2, cap, HD), BF16),
            pltpu.VMEM((unit_rows, keys), F32),
            pltpu.VMEM((unit_rows, keys), F32),
            pltpu.VMEM((3, unit_rows, HD), F32),
            pltpu.VMEM((2, 2, unit_rows, HD), F32),
            pltpu.VMEM((2, 2, unit_rows, HD), F32),
            pltpu.VMEM((2, 3, ROWS, HD), F32),
            pltpu.VMEM((chips, ROWS, HD), BF16),
            pltpu.VMEM((chips, ROWS, HD), BF16),
            pltpu.VMEM((chips, 1, HD), F32),
            pltpu.VMEM((chips, 1, HD), F32),
            pltpu.VMEM((z_chips, 2, PER_GROUP * HD), BF16),
            dma((5,)),
            dma,
            dma((x_chips,)),
            dma((x_chips,)),
            dma((x_chips,)),
            dma((2,)),
            dma((2,)),
            dma,
            dma((2,)),
            dma,
            dma((2,)),
            dma,
            dma,
        ],
        compiler_params=pltpu.CompilerParams(collective_id=0, has_side_effects=True, vmem_limit_bytes=56 << 20),
        name="attend",
    )(
        *(pltpu.with_memory_space_constraint(each, pltpu.MemorySpace.HBM) for each in arrays)
    )
    return jnp.swapaxes(heads, 0, 1).reshape(2, z_chips * PER_GROUP * HD)


def solution(mesh):
    in_specs = (
        P("seq", "head"),
        P("seq", "head"),
        P("seq", "head"),
        P("seq", None, "head"),
        P("seq", None, "head"),
        P("seq"),
        P("seq"),
    )
    return jax.shard_map(
        functools.partial(on_device, 4), mesh=mesh, in_specs=in_specs, out_specs=P("seq", None), check_vma=False
    )
```
